32 devices in a mesh: pages: 8 (over z, x), queries: 4 (over y, core).
Axes of the slice: x: 2, y: 2, z: 4, core: 2. Of those that a mesh axis runs over, the one named last changes fastest.
Arguments:
- query_tokens: bfloat16 [8, 32, 128], P('pages'), may hold values from -1 to 1
- page_patches: bfloat16 [16, 1536, 128], P('pages', 'queries'), may hold values from -1 to 1, as said below
- patch_counts: int32 [16], P('pages'), may hold values from 512 to 1536, as said below
- positive_page: int32 [8], replicated, may hold values from 0 to 15
Outputs:
- query_loss: float32 [8], replicated
- query_grad: float32 [8, 32, 128], P('pages', 'queries')
- page_grad: float32 [16, 1536, 128], P('pages', 'queries')
The draws below stay inside these ranges and needn't reach their ends.
Inputs may be any that keep to these rules, and one draw needn't show every extreme that they name: `patch_counts`: each page's number of valid patches; some page has exactly 1536. `page_patches`: slots at or past a page's count hold arbitrary values.
All inputs are finite; a program needn't handle non-finite values.
Results may differ from the reference program's by a relative error of at most 0.0028.
Values may be sent and summed in bfloat16 or wider, within the bound.
No kernel may reach another device: no remote copies, remote signals or barrier semaphores. Data moves between devices by JAX's collectives and lax.ppermute only.
A program may use at most 64 MiB of HBM per device.

```python
import jax
import jax.numpy as jnp
from jax import lax

E = 128
QT = 32
MAXP = 1536
MINP = 512
NQ = 8
NPG = 16


def layout(key):
    base_key = jax.random.fold_in(key, 7001)
    counts_all = jax.random.randint(jax.random.fold_in(base_key, 1), (NPG,), MINP, MAXP + 1)
    page_order = jax.random.permutation(jax.random.fold_in(base_key, 2), NPG)
    first = page_order[:4]
    second = page_order[4:8]
    counts_all = counts_all.at[first[0]].set(MAXP)
    counts_all = counts_all.at[second].set(counts_all[first])
    return counts_all


def page_scale():
    position = jnp.arange(NPG, dtype=jnp.float32) / NPG
    return (0.25 * jnp.exp2(position))[:, None, None]


def draw_patch_counts(key, part):
    counts_all = layout(key)
    return counts_all.astype(jnp.int32)


def draw_query_tokens(key, part):
    own_key = jax.random.fold_in(key, 11)
    values = jnp.clip(jax.random.normal(own_key, (NQ, QT, E)), -3.0, 3.0) * 0.25 / jnp.sqrt(E * 1.0)
    return values.astype(jnp.bfloat16)


def draw_page_patches(key, part):
    own_key = jax.random.fold_in(key, 13)
    values = jnp.clip(jax.random.normal(own_key, (NPG, MAXP, E)), -3.0, 3.0) * page_scale() / jnp.sqrt(E * 1.0)
    return values.astype(jnp.bfloat16)


def place_ends(entries, rng, smallest, largest):
    place = [jax.random.randint(jax.random.fold_in(rng, axis), (), 0, length) for axis, length in enumerate(entries.shape)]
    widest = entries.shape.index(max(entries.shape))
    next_to = place[:widest] + [(place[widest] + 1) % entries.shape[widest]] + place[widest + 1:]
    return entries.at[tuple(place)].set(smallest).at[tuple(next_to)].set(largest)


def setup_inputs(seed: int = 0) -> dict:
    keys = jax.random.split(jax.random.key(seed), 5)
    return {
        "query_tokens": draw_query_tokens(jax.random.fold_in(keys[4], 71), 0),
        "page_patches": draw_page_patches(jax.random.fold_in(keys[4], 71), 0),
        "patch_counts": draw_patch_counts(jax.random.fold_in(keys[4], 71), 0),
        "positive_page": place_ends(jax.random.randint(keys[3], (NQ,), 0, NPG), jax.random.fold_in(keys[3], 1), 0, NPG - 1).astype(jnp.int32),
    }


smooth_tau = 0.05
page_temp = 0.02


def page_similar(token_rows, page_rows, count_now):
    similar = jnp.dot(token_rows, page_rows.T, preferred_element_type=jnp.float32)
    valid_mask = jnp.arange(page_rows.shape[0], dtype=jnp.int32) < count_now
    masked = jnp.where(valid_mask[None, :], similar, -1e30)
    return masked, valid_mask


def reference(query_tokens, page_patches, patch_counts, positive_page):
    query_count, query_len, embed_width = query_tokens.shape
    page_total = page_patches.shape[0]
    token_rows = query_tokens.reshape(query_count * query_len, embed_width)

    def forward(item):
        page_rows, count_now = item
        masked, valid_mask = page_similar(token_rows, page_rows, count_now)
        highest = jnp.max(masked, axis=1)
        terms = jnp.where(valid_mask[None, :], jnp.exp((masked - highest[:, None]) / smooth_tau), 0.0)
        return highest + smooth_tau * jnp.log(jnp.sum(terms, axis=1))

    patch_lse = lax.map(forward, (page_patches, patch_counts))
    smooth = patch_lse - smooth_tau * jnp.log(patch_counts.astype(jnp.float32))[:, None]
    logits = smooth.reshape(page_total, query_count, query_len).sum(axis=2).T / page_temp
    highest = jnp.max(logits, axis=1)
    page_sum = jnp.sum(jnp.exp(logits - highest[:, None]), axis=1)
    is_positive = jnp.arange(page_total, dtype=jnp.int32)[None, :] == positive_page[:, None]
    query_loss = highest + jnp.log(page_sum) - jnp.sum(jnp.where(is_positive, logits, 0.0), axis=1)
    weights = (jnp.exp(logits - highest[:, None]) / page_sum[:, None] - is_positive.astype(jnp.float32)) / page_temp
    row_weights = jnp.broadcast_to(weights.T[:, :, None], (page_total, query_count, query_len)).reshape(page_total, query_count * query_len)

    def backward(grad_rows, item):
        page_rows, count_now, page_lse, page_weight = item
        masked, valid_mask = page_similar(token_rows, page_rows, count_now)
        prob_tile = jnp.where(valid_mask[None, :], jnp.exp((masked - page_lse[:, None]) / smooth_tau), 0.0)
        coef_tile = (page_weight[:, None] * prob_tile).astype(jnp.bfloat16)
        grad_rows = grad_rows + jnp.dot(coef_tile, page_rows, preferred_element_type=jnp.float32)
        page_grad = jnp.dot(coef_tile.T, token_rows, preferred_element_type=jnp.float32)
        return grad_rows, page_grad

    start_grad = jnp.zeros((query_count * query_len, embed_width), jnp.float32)
    grad_rows, page_grad = lax.scan(backward, start_grad, (page_patches, patch_counts, patch_lse, row_weights))
    return query_loss, grad_rows.reshape(query_count, query_len, embed_width), page_grad
```

```python
import functools

import jax
import jax.numpy as jnp
from jax import lax
from jax.experimental import pallas as pl
from jax.experimental.pallas import tpu as pltpu
from jax.sharding import PartitionSpec as P

smooth_tau = 0.05
page_temp = 0.02
neg_large = -1e30
inv_tau = 1.0 / smooth_tau
inv_temp = 1.0 / page_temp
lanes = 128
block_rows = 256
both = ("pages", "queries")


def contract(a, b, dim_a, dim_b):
    return lax.dot_general(
        a, b, (((dim_a,), (dim_b,)), ((), ())), preferred_element_type=jnp.float32
    )


def over_blocks(count, body):
    if count == 1:
        body(0)
    else:
        lax.fori_loop(0, count, lambda b, _: (body(b), 0)[1], 0)


def forward_kernel(sizes, counts, tokens, own, partner, out, scores):
    slots, share, chunk = sizes
    page_local, patch_local, width = own.shape
    query_len = tokens.shape[1]
    block_queries = block_rows // query_len
    block_peers = block_queries * slots // 2
    slot = lax.axis_index("queries")
    parity = lax.rem(slot, 2)
    sources = ((own, slot * patch_local), (partner, (slot + 1 - 2 * parity) * patch_local))
    position = lax.broadcasted_iota(jnp.int32, (chunk, block_rows), 0)
    steps = [
        (source, start, base, index * patch_local + start)
        for index, (source, base) in enumerate(sources)
        for start in range(0, patch_local, chunk)
    ]

    def block(b):
        query_start = pl.multiple_of(b * block_queries, block_queries)
        token_rows = tokens[pl.ds(query_start, block_queries)].reshape(block_rows, width)
        for page in range(page_local):
            count = counts[page]
            running = jnp.full((8, block_rows), neg_large, jnp.float32)
            for source, start, base, place in steps:
                similar = contract(source[page, start : start + chunk], token_rows, 1, 1)
                live = position < count - base - start
                masked = jnp.where(live, similar, neg_large)
                scores[page, place : place + chunk] = masked
                running = jnp.maximum(
                    running, jnp.max(masked.reshape(chunk // 8, 8, block_rows), axis=0)
                )
            highest = jnp.max(running, axis=0, keepdims=True)
            total = jnp.zeros((8, block_rows), jnp.float32)
            mean = jnp.zeros((width, block_rows), jnp.float32)
            for source, start, base, place in steps:
                terms = jnp.exp((scores[page, place : place + chunk] - highest) * inv_tau)
                total = total + jnp.sum(terms.reshape(chunk // 8, 8, block_rows), axis=0)
                coarse = terms.astype(jnp.bfloat16)
                fine = (terms - coarse.astype(jnp.float32)).astype(jnp.bfloat16)
                patch_rows = source[page, start : start + chunk]
                mean = mean + contract(patch_rows, coarse, 0, 0) + contract(patch_rows, fine, 0, 0)
            total = jnp.sum(total, axis=0, keepdims=True)
            any_live = count > (slot - parity) * patch_local
            log_count = jnp.log(jnp.full((1, block_rows), count, jnp.int32).astype(jnp.float32))
            smooth = highest + smooth_tau * (jnp.log(total) - log_count)
            smooth = jnp.where(any_live, smooth, neg_large)
            rows = jnp.transpose(mean / total).reshape(block_peers, 2, share, width)
            mine = jnp.where(parity == 0, rows[:, 0], rows[:, 1])
            peer_start = pl.multiple_of(b * block_peers, block_peers)
            out[pl.ds(peer_start, block_peers), page * share : (page + 1) * share] = mine
            for half in range(block_rows // lanes):
                line = page_local * share + (page * block_rows // lanes) + half
                line = line + b * (page_local * block_rows // lanes)
                part = smooth[:, half * lanes : (half + 1) * lanes]
                out[:, pl.ds(line, 1)] = jnp.broadcast_to(part[None], (out.shape[0], 1, lanes))

    over_blocks(tokens.shape[0] // block_queries, block)


def backward_kernel(sizes, counts, positive, heard, tokens, own, loss, query_grad, page_grad):
    slots, share, chunk = sizes
    page_local, patch_local, width = own.shape
    query_len = tokens.shape[1]
    block_queries = block_rows // query_len
    halves = block_rows // lanes
    half_queries = lanes // query_len
    groups = heard.shape[0] // 2
    stride = heard.shape[1]
    slot = lax.axis_index("queries")
    group = lax.axis_index("pages")
    flat = heard.reshape(heard.shape[0] * stride, lanes)
    same_query = (
        lax.broadcasted_iota(jnp.int32, (lanes, lanes), 0) // query_len
        == lax.broadcasted_iota(jnp.int32, (lanes, lanes), 1) // query_len
    ).astype(jnp.bfloat16)
    group_ids = lax.broadcasted_iota(jnp.int32, (groups, lanes), 0)
    lane_query = lax.broadcasted_iota(jnp.int32, (1, lanes), 1) // query_len
    position = lax.broadcasted_iota(jnp.int32, (chunk, block_rows), 0)
    pages = range(page_local)

    def token_sums(x):
        coarse = x.astype(jnp.bfloat16)
        rest = x - coarse.astype(jnp.float32)
        middle = rest.astype(jnp.bfloat16)
        fine = (rest - middle.astype(jnp.float32)).astype(jnp.bfloat16)
        sums = contract(jnp.concatenate([coarse, middle, fine], axis=0), same_query, 1, 0)
        size = x.shape[0]
        return sums[:size] + sums[size : 2 * size] + sums[2 * size :]

    def mine(x):
        return jnp.sum(jnp.where(group_ids == group, x, 0.0), axis=0, keepdims=True)

    def block(b):
        row_weights = [[] for _ in pages]
        row_lse = [[] for _ in pages]
        shares = []
        for half in range(halves):
            smooth = []
            parts = []
            for page in pages:
                line = page_local * share + page * halves + half + b * (page_local * halves)
                first = flat[pl.ds(line, groups, stride=2 * stride), :]
                second = flat[pl.ds(line + stride, groups, stride=2 * stride), :]
                highest = jnp.maximum(first, second)
                first = jnp.exp((first - highest) * inv_tau)
                second = jnp.exp((second - highest) * inv_tau)
                total = first + second
                smooth.append(highest + smooth_tau * jnp.log(total))
                parts.append((first / total, second / total))
            sums = token_sums(jnp.concatenate(smooth, axis=0)) * inv_temp
            logits = [sums[page * groups : (page + 1) * groups] for page in pages]
            top = functools.reduce(jnp.maximum, logits)
            top = jnp.max(top, axis=0, keepdims=True)
            grown = [jnp.exp(x - top) for x in logits]
            total = jnp.sum(functools.reduce(jnp.add, grown), axis=0, keepdims=True)
            first_query = b * block_queries + half * half_queries
            target = jnp.zeros((1, lanes), jnp.int32)
            for i in range(half_queries):
                target = jnp.where(lane_query == i, positive[first_query + i], target)
            hits = [group_ids * page_local + page == target for page in pages]
            found = functools.reduce(
                jnp.add, [jnp.where(hit, x, 0.0) for hit, x in zip(hits, logits)]
            )
            losses = top + jnp.log(total) - jnp.sum(found, axis=0, keepdims=True)
            for i in range(half_queries):
                loss[first_query + i] = jnp.max(losses[:, i * query_len : (i + 1) * query_len])
            weights = [
                (x / total - jnp.where(hit, 1.0, 0.0)) * inv_temp for hit, x in zip(hits, grown)
            ]
            for page in pages:
                row_weights[page].append(mine(weights[page]))
                row_lse[page].append(mine(smooth[page]))
            shares.append([weights[page] * part for page in pages for part in parts[page]])

        block_tokens = tokens[
            pl.ds(pl.multiple_of(b * block_queries, block_queries), block_queries)
        ].reshape(block_rows, width)
        for page in pages:
            count = counts[page]
            live_count = count - slot * patch_local
            log_count = jnp.log(jnp.full((1, block_rows), count, jnp.int32).astype(jnp.float32))
            page_weight = jnp.concatenate(row_weights[page], axis=1)
            page_lse = jnp.concatenate(row_lse[page], axis=1) + smooth_tau * log_count
            for start in range(0, patch_local, chunk):
                similar = contract(own[page, start : start + chunk], block_tokens, 1, 1)
                coef = page_weight * jnp.exp((similar - page_lse) * inv_tau)
                coef = jnp.where(position < live_count - start, coef, 0.0).astype(jnp.bfloat16)
                grad = contract(coef, block_tokens, 1, 0)
                if tokens.shape[0] > block_queries:
                    grad = grad + jnp.where(b == 0, 0.0, page_grad[page, start : start + chunk])
                page_grad[page, start : start + chunk] = grad

        @pl.when(group // block_queries == b)
        def _():
            row = lax.rem(group, block_queries) * query_len + slot * share
            half = row // lanes
            grad = jnp.zeros((share, width), jnp.float32)
            for index in range(len(shares[0])):
                page, side = index // 2, index % 2
                picked = shares[0][index]
                for other in range(1, halves):
                    picked = jnp.where(half == other, shares[other][index], picked)
                picked = pltpu.roll(picked, lax.rem(lanes - lax.rem(row, lanes), lanes), 1)
                columns = jnp.transpose(picked)[:share]
                for g in range(groups):
                    part = heard[2 * g + side, page * share : (page + 1) * share]
                    grad = grad + columns[:, g : g + 1] * part
            query_grad[0] = grad

    over_blocks(tokens.shape[0] // block_queries, block)


def shards(page_groups, slots, query_tokens, page_patches, patch_counts, positive_page):
    query_local, query_len, width = query_tokens.shape
    page_local, patch_local, _ = page_patches.shape
    query_count = query_local * page_groups
    share = query_len // slots
    chunk = 128
    lines = page_local * share + page_local * query_count * query_len // lanes
    lines = -(-lines // 8) * 8
    peers = page_groups * slots // 2
    sizes = (slots, share, chunk)
    smem = pl.BlockSpec(memory_space=pltpu.SMEM)
    vmem = pl.BlockSpec(memory_space=pltpu.VMEM)
    limit = (16 << 20) + 2 * peers * lines * lanes * 4
    params = pltpu.CompilerParams(vmem_limit_bytes=limit)

    partner = lax.ppermute(page_patches, "queries", [(i, i ^ 1) for i in range(slots)])
    tokens = lax.all_to_all(
        jnp.broadcast_to(query_tokens, (page_groups, query_len, width)), "pages", 0, 0, tiled=True
    )
    told = pl.pallas_call(
        functools.partial(forward_kernel, sizes),
        out_shape=jax.ShapeDtypeStruct((peers, lines, lanes), jnp.float32),
        in_specs=[smem, vmem, vmem, vmem],
        out_specs=vmem,
        scratch_shapes=[pltpu.VMEM((page_local, 2 * patch_local, block_rows), jnp.float32)],
        compiler_params=params,
        name="forward",
    )(patch_counts, tokens, page_patches, partner)
    members = [
        [g * slots + k for g in range(page_groups) for k in range(parity, slots, 2)]
        for parity in range(2)
    ]
    heard = lax.all_to_all(told, both, 0, 0, axis_index_groups=members, tiled=True)
    return pl.pallas_call(
        functools.partial(backward_kernel, sizes),
        out_shape=(
            jax.ShapeDtypeStruct((query_count,), jnp.float32),
            jax.ShapeDtypeStruct((query_local, share, width), jnp.float32),
            jax.ShapeDtypeStruct((page_local, patch_local, width), jnp.float32),
        ),
        in_specs=[smem, smem, vmem, vmem, vmem],
        out_specs=(smem, vmem, vmem),
        compiler_params=params,
        name="backward",
    )(patch_counts, positive_page, heard, tokens, page_patches)


def solution(mesh):
    in_specs = (P("pages", None, None), P("pages", "queries", None), P("pages"), P())
    out_specs = (P(), P("pages", "queries", None), P("pages", "queries", None))
    body = functools.partial(shards, mesh.shape["pages"], mesh.shape["queries"])
    return jax.shard_map(body, mesh=mesh, in_specs=in_specs, out_specs=out_specs, check_vma=False)
```

```python
import functools
import math

import jax
import jax.numpy as jnp
from jax import lax
from jax.experimental import pallas as pl
from jax.experimental.pallas import tpu as pltpu
from jax.sharding import PartitionSpec as P

smooth_tau = 0.05
page_temp = 0.02
neg_large = -1e30
inv_tau = 1.0 / smooth_tau
inv_temp = 1.0 / page_temp
lanes = 128
block_rows = 256
chunk = 128
both = ("pages", "queries")


def contract(a, b, dim_a, dim_b):
    return lax.dot_general(
        a, b, (((dim_a,), (dim_b,)), ((), ())), preferred_element_type=jnp.float32
    )


def over_blocks(count, body):
    if count == 1:
        body(0)
    else:
        lax.fori_loop(0, count, lambda b, _: (body(b), 0)[1], 0)


def block_of_tokens(tokens, b):
    count = block_rows // tokens.shape[1]
    start = pl.multiple_of(b * count, count)
    return tokens[pl.ds(start, count)].reshape(block_rows, tokens.shape[2])


def integer_rows(counts, positive, rows):
    counts, positive = counts[...][None], positive[...][None]
    lists = [jnp.broadcast_to(counts[:, i : i + 1], (1, rows)) for i in range(counts.shape[1])]
    query_count = positive.shape[1]
    row_query = lax.broadcasted_iota(jnp.int32, (1, rows), 1) // (rows // query_count)
    target = jnp.zeros((1, rows), jnp.int32)
    for query in range(query_count):
        target = jnp.where(row_query == query, positive[:, query : query + 1], target)
    return jnp.concatenate([*lists, target], axis=0)


def log_row(count):
    return jnp.log(count.astype(jnp.float32))


def forward_kernel(share, lines, counts, positive, tokens, own, partner, out, integers, scores):
    page_local, patch_local, width = own.shape
    halves = block_rows // lanes
    block_peers = block_rows // share
    peers = out.shape[0] // lines
    pair_pages = page_local // 2
    slot = lax.axis_index("queries")
    parity = lax.rem(slot, 2)
    sources = ((own, slot * patch_local), (partner, (slot + 1 - 2 * parity) * patch_local))
    position = lax.broadcasted_iota(jnp.int32, (chunk, block_rows), 0)
    steps = [
        (source, start, base, index * patch_local + start)
        for index, (source, base) in enumerate(sources)
        for start in range(0, patch_local, chunk)
    ]

    integers[...] = integer_rows(counts, positive, integers.shape[1])

    def block(b):
        token_rows = block_of_tokens(tokens, b)
        for index in range(pair_pages):
            page = parity * pair_pages + index
            count = integers[pl.ds(page, 1), :block_rows]
            running = jnp.full((8, block_rows), neg_large, jnp.float32)
            for source, start, base, place in steps:
                similar = contract(source[page, start : start + chunk], token_rows, 1, 1)
                live = position < count - base - start
                masked = jnp.where(live, similar, neg_large)
                scores[place : place + chunk] = masked
                running = jnp.maximum(
                    running, jnp.max(masked.reshape(chunk // 8, 8, block_rows), axis=0)
                )
            highest = jnp.max(running, axis=0, keepdims=True)
            total = jnp.zeros((8, block_rows), jnp.float32)
            mean = jnp.zeros((width, block_rows), jnp.float32)
            for source, start, base, place in steps:
                terms = jnp.exp((scores[place : place + chunk] - highest) * inv_tau)
                total = total + jnp.sum(terms.reshape(chunk // 8, 8, block_rows), axis=0)
                coarse = terms.astype(jnp.bfloat16)
                fine = (terms - coarse.astype(jnp.float32)).astype(jnp.bfloat16)
                patch_rows = source[page, start : start + chunk]
                mean = mean + contract(patch_rows, coarse, 0, 0) + contract(patch_rows, fine, 0, 0)
            total = jnp.sum(total, axis=0, keepdims=True)
            any_live = count > (slot - parity) * patch_local
            smooth = highest + smooth_tau * (jnp.log(total) - log_row(count))
            smooth = jnp.where(any_live, smooth, neg_large)
            rows = jnp.transpose(mean / total)
            for i in range(block_peers):
                line = (b * block_peers + i) * lines + index * share
                out[pl.ds(line, share)] = rows[i * share : (i + 1) * share]
            for half in range(halves):
                line = pair_pages * share + (b * pair_pages + index) * halves + half
                part = smooth[:, half * lanes : (half + 1) * lanes]
                out[pl.ds(line, peers, stride=lines)] = jnp.broadcast_to(part, (peers, lanes))

    over_blocks(tokens.shape[0] * tokens.shape[1] // block_rows, block)


def backward_kernel(
    slots, share, lines, integers, heard, tokens, own, loss, query_grad, page_grad
):
    page_local, patch_local, width = own.shape
    query_len = tokens.shape[1]
    block_queries = block_rows // query_len
    halves = block_rows // lanes
    half_queries = lanes // query_len
    pair_pages = page_local // 2
    groups = heard.shape[0] // (lines * slots)
    sides = slots // 2
    slot = lax.axis_index("queries")
    group = lax.axis_index("pages")
    same_query = (
        lax.broadcasted_iota(jnp.int32, (lanes, lanes), 0) // query_len
        == lax.broadcasted_iota(jnp.int32, (lanes, lanes), 1) // query_len
    ).astype(jnp.bfloat16)
    group_ids = lax.broadcasted_iota(jnp.int32, (groups, lanes), 0)
    position = lax.broadcasted_iota(jnp.int32, (chunk, block_rows), 0)
    pages = range(page_local)

    def sender(page, side):
        return 2 * side + page // pair_pages

    def token_sums(x):
        coarse = x.astype(jnp.bfloat16)
        rest = x - coarse.astype(jnp.float32)
        middle = rest.astype(jnp.bfloat16)
        fine = (rest - middle.astype(jnp.float32)).astype(jnp.bfloat16)
        sums = contract(jnp.concatenate([coarse, middle, fine], axis=0), same_query, 1, 0)
        size = x.shape[0]
        return sums[:size] + sums[size : 2 * size] + sums[2 * size :]

    def mine(x):
        return jnp.sum(jnp.where(group_ids == group, x, 0.0), axis=0, keepdims=True)

    def block(b):
        row_weights = [[] for _ in pages]
        row_lse = [[] for _ in pages]
        shares = []
        for half in range(halves):
            smooth = []
            parts = []
            for page in pages:
                line = pair_pages * share + (b * pair_pages + page % pair_pages) * halves + half
                heights = [
                    heard[pl.ds(sender(page, side) * lines + line, groups, stride=slots * lines)]
                    for side in range(sides)
                ]
                highest = functools.reduce(jnp.maximum, heights)
                terms = [jnp.exp((x - highest) * inv_tau) for x in heights]
                total = functools.reduce(jnp.add, terms)
                smooth.append(highest + smooth_tau * jnp.log(total))
                parts.append([x / total for x in terms])
            sums = token_sums(jnp.concatenate(smooth, axis=0)) * inv_temp
            logits = [sums[page * groups : (page + 1) * groups] for page in pages]
            top = functools.reduce(jnp.maximum, logits)
            top = jnp.max(top, axis=0, keepdims=True)
            grown = [jnp.exp(x - top) for x in logits]
            total = jnp.sum(functools.reduce(jnp.add, grown), axis=0, keepdims=True)
            first_query = b * block_queries + half * half_queries
            line = pl.multiple_of(first_query * query_len, lanes)
            target = integers[page_local : page_local + 1, pl.ds(line, lanes)]
            hits = [group_ids * page_local + page == target for page in pages]
            found = functools.reduce(
                jnp.add, [jnp.where(hit, x, 0.0) for hit, x in zip(hits, logits)]
            )
            losses = top + jnp.log(total) - jnp.sum(found, axis=0, keepdims=True)
            for i in range(half_queries):
                loss[first_query + i] = jnp.max(losses[:, i * query_len : (i + 1) * query_len])
            weights = [
                (x / total - jnp.where(hit, 1.0, 0.0)) * inv_temp for hit, x in zip(hits, grown)
            ]
            for page in pages:
                row_weights[page].append(mine(weights[page]))
                row_lse[page].append(mine(smooth[page]))
            shares.append([[weights[page] * part for part in parts[page]] for page in pages])

        token_rows = block_of_tokens(tokens, b)
        for page in pages:
            count = integers[page : page + 1, :block_rows]
            live_count = count - slot * patch_local
            page_weight = jnp.concatenate(row_weights[page], axis=1)
            page_lse = jnp.concatenate(row_lse[page], axis=1) + smooth_tau * log_row(count)
            for start in range(0, patch_local, chunk):
                similar = contract(own[page, start : start + chunk], token_rows, 1, 1)
                coef = page_weight * jnp.exp((similar - page_lse) * inv_tau)
                coef = jnp.where(position < live_count - start, coef, 0.0).astype(jnp.bfloat16)
                grad = contract(coef, token_rows, 1, 0)
                if tokens.shape[0] > block_queries:
                    grad = grad + jnp.where(b == 0, 0.0, page_grad[page, start : start + chunk])
                page_grad[page, start : start + chunk] = grad

        @pl.when(group // block_queries == b)
        def _():
            row = lax.rem(group, block_queries) * query_len + slot * share
            half = row // lanes
            grad = jnp.zeros((share, width), jnp.float32)
            for page in pages:
                for side in range(sides):
                    picked = shares[0][page][side]
                    for other in range(1, halves):
                        picked = jnp.where(half == other, shares[other][page][side], picked)
                    picked = pltpu.roll(picked, lax.rem(lanes - lax.rem(row, lanes), lanes), 1)
                    columns = jnp.transpose(picked)[:share]
                    for g in range(groups):
                        line = (g * slots + sender(page, side)) * lines
                        line = line + page % pair_pages * share
                        grad = grad + columns[:, g : g + 1] * heard[line : line + share]
            query_grad[0] = grad

    over_blocks(tokens.shape[0] // block_queries, block)


def shards(page_groups, slots, query_tokens, page_patches, patch_counts, positive_page):
    query_local, query_len, width = query_tokens.shape
    page_local, patch_local, _ = page_patches.shape
    query_count = query_local * page_groups
    share = query_len // slots
    peers = page_groups * slots
    lines = page_local // 2 * (share + query_count * query_len // lanes)
    tile = math.gcd(lines, 8)
    smem = pl.BlockSpec(memory_space=pltpu.SMEM)
    vmem = pl.BlockSpec(memory_space=pltpu.VMEM)
    limit = (16 << 20) + 2 * peers * lines * lanes * 4
    params = pltpu.CompilerParams(vmem_limit_bytes=limit)

    partner = lax.ppermute(page_patches, "queries", [(i, i ^ 1) for i in range(slots)])
    tokens = lax.all_to_all(
        jnp.broadcast_to(query_tokens, (page_groups, query_len, width)), "pages", 0, 0, tiled=True
    )
    told, integers = pl.pallas_call(
        functools.partial(forward_kernel, share, lines),
        out_shape=(
            jax.ShapeDtypeStruct((peers * lines, lanes), jnp.float32),
            jax.ShapeDtypeStruct((page_local + 1, query_count * query_len), jnp.int32),
        ),
        in_specs=[vmem] * 5,
        out_specs=(vmem, vmem),
        scratch_shapes=[pltpu.VMEM((2 * patch_local, block_rows), jnp.float32)],
        compiler_params=params,
        name="forward",
    )(patch_counts, positive_page, tokens, page_patches, partner)
    told = told.reshape(peers, lines // tile, tile, lanes)
    heard = lax.all_to_all(told, both, 0, 0, tiled=True).reshape(peers * lines, lanes)
    return pl.pallas_call(
        functools.partial(backward_kernel, slots, share, lines),
        out_shape=(
            jax.ShapeDtypeStruct((query_count,), jnp.float32),
            jax.ShapeDtypeStruct((query_local, share, width), jnp.float32),
            jax.ShapeDtypeStruct((page_local, patch_local, width), jnp.float32),
        ),
        in_specs=[vmem] * 4,
        out_specs=(smem, vmem, vmem),
        compiler_params=params,
        name="backward",
    )(integers, heard, tokens, page_patches)


def solution(mesh):
    in_specs = (P("pages", None, None), P("pages", "queries", None), P("pages"), P())
    out_specs = (P(), P("pages", "queries", None), P("pages", "queries", None))
    body = functools.partial(shards, mesh.shape["pages"], mesh.shape["queries"])
    return jax.shard_map(body, mesh=mesh, in_specs=in_specs, out_specs=out_specs, check_vma=False)
```

```python
import functools
import math

import jax
import jax.numpy as jnp
from jax import lax
from jax.experimental import pallas as pl
from jax.experimental.pallas import tpu as pltpu
from jax.sharding import PartitionSpec as P

smooth_tau = 0.05
page_temp = 0.02
neg_large = -1e30
inv_tau = 1.0 / smooth_tau
inv_temp = 1.0 / page_temp
inv_tau_log2 = inv_tau / math.log(2.0)
lanes = 128
block_rows = 256
chunk = 128
both = ("pages", "queries")


def contract(a, b, dim_a, dim_b):
    return lax.dot_general(
        a, b, (((dim_a,), (dim_b,)), ((), ())), preferred_element_type=jnp.float32
    )


def over_blocks(count, body):
    if count == 1:
        body(0)
    else:
        lax.fori_loop(0, count, lambda b, _: (body(b), 0)[1], 0)


def block_of_tokens(tokens, b):
    count = block_rows // tokens.shape[1]
    start = pl.multiple_of(b * count, count)
    return tokens[pl.ds(start, count)].reshape(block_rows, tokens.shape[2])


def integer_rows(counts, positive, rows):
    counts, positive = counts[...][None], positive[...][None]
    lists = [jnp.broadcast_to(counts[:, i : i + 1], (1, rows)) for i in range(counts.shape[1])]
    query_count = positive.shape[1]
    row_query = lax.broadcasted_iota(jnp.int32, (1, rows), 1) // (rows // query_count)
    target = jnp.zeros((1, rows), jnp.int32)
    for query in range(query_count):
        target = jnp.where(row_query == query, positive[:, query : query + 1], target)
    return jnp.concatenate([*lists, target], axis=0)


def log_row(count):
    return jnp.log(count.astype(jnp.float32))


def forward_kernel(
    share, lines, counts, positive, tokens, own, partner, out, integers, scores
):
    page_local, patch_local, width = own.shape
    block_peers = block_rows // share
    peers = out.shape[0] // lines
    pair_pages = page_local // 2
    slot = lax.axis_index("queries")
    parity = lax.rem(slot, 2)
    sources = ((own, slot * patch_local), (partner, (slot + 1 - 2 * parity) * patch_local))
    position = lax.broadcasted_iota(jnp.int32, (1, lanes), 1)
    diagonal = lax.broadcasted_iota(jnp.int32, (lanes, lanes), 0) == lax.broadcasted_iota(
        jnp.int32, (lanes, lanes), 1
    )
    places = [slice(start, start + lanes) for start in range(0, patch_local, lanes)]
    integers[...] = integer_rows(counts, positive, integers.shape[1])

    def as_row(column):
        return jnp.sum(jnp.where(diagonal, column, 0.0), axis=0, keepdims=True)

    def block(b):
        token_rows = block_of_tokens(tokens, b)
        for index in range(pair_pages):
            page = parity * pair_pages + index
            count = integers[pl.ds(page, 1), :block_rows][:, :lanes]
            running = jnp.full((block_rows, lanes), neg_large, jnp.float32)
            for turn, (source, base) in enumerate(sources):
                similar = contract(token_rows, source[page], 1, 1)
                for place in places:
                    live = position < count - base - place.start
                    live = jnp.broadcast_to(live, (block_rows, lanes))
                    masked = jnp.where(live, similar[:, place], neg_large)
                    scores[turn, :, place] = masked
                    running = jnp.maximum(running, masked)
            highest = jnp.max(running, axis=1, keepdims=True)
            total = jnp.zeros((block_rows, lanes), jnp.float32)
            mean = jnp.zeros((block_rows, width), jnp.float32)
            for turn, (source, base) in enumerate(sources):
                coarse, fine = [], []
                for place in places:
                    terms = jnp.exp2((scores[turn, :, place] - highest) * inv_tau_log2)
                    total = total + terms
                    coarse.append(terms.astype(jnp.bfloat16))
                    fine.append((terms - coarse[-1].astype(jnp.float32)).astype(jnp.bfloat16))
                for part in (coarse, fine):
                    mean = mean + contract(jnp.concatenate(part, axis=1), source[page], 1, 0)
            total = jnp.sum(total, axis=1, keepdims=True)
            mean = mean * (1.0 / total)
            for i in range(block_peers):
                line = (b * block_peers + i) * lines + index * share
                out[pl.ds(line, share)] = mean[i * share : (i + 1) * share]
            any_live = count > (slot - parity) * patch_local
            log_count = jnp.log(count.astype(jnp.float32))
            for half in range(block_rows // lanes):
                rows = slice(half * lanes, (half + 1) * lanes)
                log_mean = jnp.log(as_row(total[rows])) - log_count
                smooth = as_row(highest[rows]) + smooth_tau * log_mean
                smooth = jnp.where(any_live, smooth, neg_large)
                line = pair_pages * share + (b * pair_pages + index) * (block_rows // lanes) + half
                out[pl.ds(line, peers, stride=lines)] = jnp.broadcast_to(smooth, (peers, lanes))

    over_blocks(tokens.shape[0] * tokens.shape[1] // block_rows, block)


def backward_kernel(
    slots, share, lines, integers, heard, tokens, own, loss, query_grad, page_grad
):
    page_local, patch_local, width = own.shape
    query_len = tokens.shape[1]
    block_queries = block_rows // query_len
    halves = block_rows // lanes
    half_queries = lanes // query_len
    pair_pages = page_local // 2
    groups = heard.shape[0] // (lines * slots)
    sides = slots // 2
    slot = lax.axis_index("queries")
    group = lax.axis_index("pages")
    same_query = (
        lax.broadcasted_iota(jnp.int32, (lanes, lanes), 0) // query_len
        == lax.broadcasted_iota(jnp.int32, (lanes, lanes), 1) // query_len
    ).astype(jnp.bfloat16)
    group_ids = lax.broadcasted_iota(jnp.int32, (groups, lanes), 0)
    position = lax.broadcasted_iota(jnp.int32, (chunk, block_rows), 0)
    pages = range(page_local)

    def sender(page, side):
        return 2 * side + page // pair_pages

    def token_sums(x):
        coarse = x.astype(jnp.bfloat16)
        rest = x - coarse.astype(jnp.float32)
        middle = rest.astype(jnp.bfloat16)
        fine = (rest - middle.astype(jnp.float32)).astype(jnp.bfloat16)
        sums = contract(jnp.concatenate([coarse, middle, fine], axis=0), same_query, 1, 0)
        size = x.shape[0]
        return sums[:size] + sums[size : 2 * size] + sums[2 * size :]

    def mine(x):
        return jnp.sum(jnp.where(group_ids == group, x, 0.0), axis=0, keepdims=True)

    def block(b):
        row_weights = [[] for _ in pages]
        row_lse = [[] for _ in pages]
        shares = []
        for half in range(halves):
            smooth = []
            parts = []
            for page in pages:
                line = pair_pages * share + (b * pair_pages + page % pair_pages) * halves + half
                heights = [
                    heard[pl.ds(sender(page, side) * lines + line, groups, stride=slots * lines)]
                    for side in range(sides)
                ]
                highest = functools.reduce(jnp.maximum, heights)
                terms = [jnp.exp2((x - highest) * inv_tau_log2) for x in heights]
                total = functools.reduce(jnp.add, terms)
                smooth.append(highest + smooth_tau * jnp.log(total))
                parts.append([x / total for x in terms])
            sums = token_sums(jnp.concatenate(smooth, axis=0)) * inv_temp
            logits = [sums[page * groups : (page + 1) * groups] for page in pages]
            top = functools.reduce(jnp.maximum, logits)
            top = jnp.max(top, axis=0, keepdims=True)
            grown = [jnp.exp(x - top) for x in logits]
            total = jnp.sum(functools.reduce(jnp.add, grown), axis=0, keepdims=True)
            first_query = b * block_queries + half * half_queries
            line = pl.multiple_of(first_query * query_len, lanes)
            target = integers[page_local : page_local + 1, pl.ds(line, lanes)]
            hits = [group_ids * page_local + page == target for page in pages]
            found = functools.reduce(
                jnp.add, [jnp.where(hit, x, 0.0) for hit, x in zip(hits, logits)]
            )
            losses = top + jnp.log(total) - jnp.sum(found, axis=0, keepdims=True)
            for i in range(half_queries):
                loss[first_query + i] = jnp.max(losses[:, i * query_len : (i + 1) * query_len])
            weights = [
                (x / total - jnp.where(hit, 1.0, 0.0)) * inv_temp for hit, x in zip(hits, grown)
            ]
            for page in pages:
                row_weights[page].append(mine(weights[page]))
                row_lse[page].append(mine(smooth[page]))
            shares.append([[weights[page] * part for part in parts[page]] for page in pages])

        token_rows = block_of_tokens(tokens, b)
        for page in pages:
            count = integers[page : page + 1, :block_rows]
            live_count = count - slot * patch_local
            page_weight = jnp.concatenate(row_weights[page], axis=1)
            page_lse = jnp.concatenate(row_lse[page], axis=1) + smooth_tau * log_row(count)
            for start in range(0, patch_local, chunk):
                similar = contract(own[page, start : start + chunk], token_rows, 1, 1)
                coef = page_weight * jnp.exp2((similar - page_lse) * inv_tau_log2)
                coef = jnp.where(position < live_count - start, coef, 0.0).astype(jnp.bfloat16)
                grad = contract(coef, token_rows, 1, 0)
                if tokens.shape[0] > block_queries:
                    grad = grad + jnp.where(b == 0, 0.0, page_grad[page, start : start + chunk])
                page_grad[page, start : start + chunk] = grad

        def own_rows():
            row = lax.rem(group, block_queries) * query_len + slot * share
            picked = []
            for page in pages:
                for side in range(sides):
                    x = shares[0][page][side]
                    for other in range(1, halves):
                        x = jnp.where(row // lanes == other, shares[other][page][side], x)
                    picked.append(x)
            picked = jnp.concatenate(picked, axis=0)
            picked = pltpu.roll(picked, lax.rem(lanes - lax.rem(row, lanes), lanes), 1)
            columns = jnp.transpose(picked)[:share]
            grads = []
            for page in pages:
                for side in range(sides):
                    place = len(grads) * groups
                    first = sender(page, side) * lines + page % pair_pages * share
                    terms = [
                        columns[:, place + g : place + g + 1]
                        * heard[first + g * slots * lines : first + g * slots * lines + share]
                        for g in range(groups)
                    ]
                    grads.append(functools.reduce(jnp.add, terms))
            query_grad[0] = functools.reduce(jnp.add, grads)

        if tokens.shape[0] == block_queries:
            own_rows()
        else:
            pl.when(group // block_queries == b)(own_rows)

    over_blocks(tokens.shape[0] // block_queries, block)


def shards(page_groups, slots, query_tokens, page_patches, patch_counts, positive_page):
    query_local, query_len, width = query_tokens.shape
    page_local, patch_local, _ = page_patches.shape
    query_count = query_local * page_groups
    share = query_len // slots
    peers = page_groups * slots
    lines = page_local // 2 * (share + query_count * query_len // lanes)
    tile = math.gcd(lines, 8)
    smem = pl.BlockSpec(memory_space=pltpu.SMEM)
    vmem = pl.BlockSpec(memory_space=pltpu.VMEM)
    limit = (16 << 20) + 2 * peers * lines * lanes * 4
    params = pltpu.CompilerParams(vmem_limit_bytes=limit)

    partner = lax.ppermute(page_patches, "queries", [(i, i ^ 1) for i in range(slots)])
    tokens = lax.all_to_all(
        jnp.broadcast_to(query_tokens, (page_groups, query_len, width)), "pages", 0, 0, tiled=True
    )
    told, integers = pl.pallas_call(
        functools.partial(forward_kernel, share, lines),
        out_shape=(
            jax.ShapeDtypeStruct((peers * lines, lanes), jnp.float32),
            jax.ShapeDtypeStruct((page_local + 1, query_count * query_len), jnp.int32),
        ),
        in_specs=[vmem] * 5,
        out_specs=(vmem, vmem),
        scratch_shapes=[pltpu.VMEM((2, block_rows, patch_local), jnp.float32)],
        compiler_params=params,
        name="forward",
    )(patch_counts, positive_page, tokens, page_patches, partner)
    told = told.reshape(peers, lines // tile, tile, lanes)
    heard = lax.all_to_all(told, both, 0, 0, tiled=True).reshape(peers * lines, lanes)
    return pl.pallas_call(
        functools.partial(backward_kernel, slots, share, lines),
        out_shape=(
            jax.ShapeDtypeStruct((query_count,), jnp.float32),
            jax.ShapeDtypeStruct((query_local, share, width), jnp.float32),
            jax.ShapeDtypeStruct((page_local, patch_local, width), jnp.float32),
        ),
        in_specs=[vmem] * 4,
        out_specs=(smem, vmem, vmem),
        compiler_params=params,
        name="backward",
    )(integers, heard, tokens, page_patches)


def solution(mesh):
    in_specs = (P("pages", None, None), P("pages", "queries", None), P("pages"), P())
    out_specs = (P(), P("pages", "queries", None), P("pages", "queries", None))
    body = functools.partial(shards, mesh.shape["pages"], mesh.shape["queries"])
    return jax.shard_map(body, mesh=mesh, in_specs=in_specs, out_specs=out_specs, check_vma=False)
```

```python
import functools
import math

import jax
import jax.numpy as jnp
from jax import lax
from jax.experimental import pallas as pl
from jax.experimental.pallas import tpu as pltpu
from jax.sharding import PartitionSpec as P

smooth_tau = 0.05
page_temp = 0.02
neg_large = -1e30
inv_tau = 1.0 / smooth_tau
inv_temp = 1.0 / page_temp
inv_tau_log2 = inv_tau / math.log(2.0)
lanes = 128
block_rows = 256
chunk = 128
both = ("pages", "queries")
fetches = ((6, 7, 2, 0), (5, 3, 1, 4))


def contract(a, b, dim_a, dim_b):
    return lax.dot_general(
        a, b, (((dim_a,), (dim_b,)), ((), ())), preferred_element_type=jnp.float32
    )


def over_blocks(count, body):
    if count == 1:
        body(0)
    else:
        lax.fori_loop(0, count, lambda b, _: (body(b), 0)[1], 0)


def block_of_tokens(tokens, b):
    count = block_rows // tokens.shape[1]
    start = pl.multiple_of(b * count, count)
    return tokens[pl.ds(start, count)].reshape(block_rows, tokens.shape[2])


def log_row(count):
    return jnp.log(count.astype(jnp.float32))


def integer_rows(counts, positive, integers):
    counts, positive = counts[...][None], positive[...][None]
    page_local = counts.shape[1]
    rows = integers.shape[1]
    for page in range(page_local):
        integers[page : page + 1] = jnp.broadcast_to(counts[:, page : page + 1], (1, rows))
    query_count = positive.shape[1]
    row_query = lax.broadcasted_iota(jnp.int32, (1, rows), 1) // (rows // query_count)
    target = jnp.zeros((1, rows), jnp.int32)
    for query in range(query_count):
        target = jnp.where(row_query == query, positive[:, query : query + 1], target)
    integers[page_local : page_local + 1] = target


def hold_kernel(patches, out):
    out[...] = patches[...]


def gather_kernel(counts, positive, _, tokens, *refs):
    fetched, (gathered, mine, integers) = refs[:-3], refs[-3:]
    integer_rows(counts, positive, integers)
    mine[...] = tokens[...]
    for i, ref in enumerate(fetched):
        gathered[i] = ref[0]


def assembled_kernel(share, lines, integers, own, partner, mine, *refs):
    slots = len(fetches[0])
    fetched, others, (out, tokens, scores) = refs[:slots], refs[slots], refs[slots + 1 :]
    group = lax.axis_index("pages")
    parity = lax.rem(lax.axis_index("queries"), 2)
    tokens[pl.ds(group, 1)] = mine[...]
    for side in range(2):
        for i, shift in enumerate(fetches[side]):
            if shift:
                block = jnp.where(parity == side, fetched[i][...], others[i : i + 1])
                tokens[pl.ds(group ^ shift, 1)] = block
    forward_kernel(share, lines, integers, tokens, own, partner, out, scores)


def forward_kernel(share, lines, integers, tokens, own, partner, out, scores):
    page_local, patch_local, width = own.shape
    block_peers = block_rows // share
    peers = out.shape[0] // lines
    pair_pages = page_local // 2
    slot = lax.axis_index("queries")
    parity = lax.rem(slot, 2)
    sources = ((own, slot * patch_local), (partner, (slot + 1 - 2 * parity) * patch_local))
    position = lax.broadcasted_iota(jnp.int32, (1, lanes), 1)
    diagonal = lax.broadcasted_iota(jnp.int32, (lanes, lanes), 0) == lax.broadcasted_iota(
        jnp.int32, (lanes, lanes), 1
    )
    places = [slice(start, start + lanes) for start in range(0, patch_local, lanes)]

    def as_row(column):
        return jnp.sum(jnp.where(diagonal, column, 0.0), axis=0, keepdims=True)

    def block(b):
        token_rows = block_of_tokens(tokens, b)
        for index in range(pair_pages):
            page = parity * pair_pages + index
            count = integers[pl.ds(page, 1), :block_rows][:, :lanes]
            running = jnp.full((block_rows, lanes), neg_large, jnp.float32)
            for turn, (source, base) in enumerate(sources):
                similar = contract(token_rows, source[page], 1, 1)
                for place in places:
                    live = position < count - base - place.start
                    live = jnp.broadcast_to(live, (block_rows, lanes))
                    masked = jnp.where(live, similar[:, place], neg_large)
                    scores[turn, :, place] = masked
                    running = jnp.maximum(running, masked)
            highest = jnp.max(running, axis=1, keepdims=True)
            total = jnp.zeros((block_rows, lanes), jnp.float32)
            mean = jnp.zeros((block_rows, width), jnp.float32)
            for turn, (source, base) in enumerate(sources):
                coarse, fine = [], []
                for place in places:
                    terms = jnp.exp2((scores[turn, :, place] - highest) * inv_tau_log2)
                    total = total + terms
                    coarse.append(terms.astype(jnp.bfloat16))
                    fine.append((terms - coarse[-1].astype(jnp.float32)).astype(jnp.bfloat16))
                for part in (coarse, fine):
                    mean = mean + contract(jnp.concatenate(part, axis=1), source[page], 1, 0)
            total = jnp.sum(total, axis=1, keepdims=True)
            mean = mean * (1.0 / total)
            for i in range(block_peers):
                line = (b * block_peers + i) * lines + index * share
                out[pl.ds(line, share)] = mean[i * share : (i + 1) * share]
            any_live = count > (slot - parity) * patch_local
            log_count = jnp.log(count.astype(jnp.float32))
            for half in range(block_rows // lanes):
                rows = slice(half * lanes, (half + 1) * lanes)
                log_mean = jnp.log(as_row(total[rows])) - log_count
                smooth = as_row(highest[rows]) + smooth_tau * log_mean
                smooth = jnp.where(any_live, smooth, neg_large)
                line = pair_pages * share + (b * pair_pages + index) * (block_rows // lanes) + half
                out[pl.ds(line, peers, stride=lines)] = jnp.broadcast_to(smooth, (peers, lanes))

    over_blocks(tokens.shape[0] * tokens.shape[1] // block_rows, block)


def backward_kernel(
    slots, share, lines, integers, heard, tokens, own, loss, query_grad, page_grad
):
    page_local, patch_local, width = own.shape
    query_len = tokens.shape[1]
    block_queries = block_rows // query_len
    halves = block_rows // lanes
    half_queries = lanes // query_len
    pair_pages = page_local // 2
    groups = heard.shape[0] // (lines * slots)
    sides = slots // 2
    slot = lax.axis_index("queries")
    group = lax.axis_index("pages")
    same_query = (
        lax.broadcasted_iota(jnp.int32, (lanes, lanes), 0) // query_len
        == lax.broadcasted_iota(jnp.int32, (lanes, lanes), 1) // query_len
    ).astype(jnp.bfloat16)
    group_ids = lax.broadcasted_iota(jnp.int32, (groups, lanes), 0)
    position = lax.broadcasted_iota(jnp.int32, (chunk, block_rows), 0)
    pages = range(page_local)

    def sender(page, side):
        return 2 * side + page // pair_pages

    def token_sums(x):
        coarse = x.astype(jnp.bfloat16)
        rest = x - coarse.astype(jnp.float32)
        middle = rest.astype(jnp.bfloat16)
        fine = (rest - middle.astype(jnp.float32)).astype(jnp.bfloat16)
        sums = contract(jnp.concatenate([coarse, middle, fine], axis=0), same_query, 1, 0)
        size = x.shape[0]
        return sums[:size] + sums[size : 2 * size] + sums[2 * size :]

    def mine(x):
        return jnp.sum(jnp.where(group_ids == group, x, 0.0), axis=0, keepdims=True)

    def block(b):
        row_weights = [[] for _ in pages]
        row_lse = [[] for _ in pages]
        shares = []
        for half in range(halves):
            smooth = []
            parts = []
            for page in pages:
                line = pair_pages * share + (b * pair_pages + page % pair_pages) * halves + half
                heights = [
                    heard[pl.ds(sender(page, side) * lines + line, groups, stride=slots * lines)]
                    for side in range(sides)
                ]
                highest = functools.reduce(jnp.maximum, heights)
                terms = [jnp.exp2((x - highest) * inv_tau_log2) for x in heights]
                total = functools.reduce(jnp.add, terms)
                smooth.append(highest + smooth_tau * jnp.log(total))
                parts.append([x / total for x in terms])
            sums = token_sums(jnp.concatenate(smooth, axis=0)) * inv_temp
            logits = [sums[page * groups : (page + 1) * groups] for page in pages]
            top = functools.reduce(jnp.maximum, logits)
            top = jnp.max(top, axis=0, keepdims=True)
            grown = [jnp.exp(x - top) for x in logits]
            total = jnp.sum(functools.reduce(jnp.add, grown), axis=0, keepdims=True)
            first_query = b * block_queries + half * half_queries
            line = pl.multiple_of(first_query * query_len, lanes)
            target = integers[page_local : page_local + 1, pl.ds(line, lanes)]
            hits = [group_ids * page_local + page == target for page in pages]
            found = functools.reduce(
                jnp.add, [jnp.where(hit, x, 0.0) for hit, x in zip(hits, logits)]
            )
            losses = top + jnp.log(total) - jnp.sum(found, axis=0, keepdims=True)
            for i in range(half_queries):
                loss[first_query + i] = jnp.max(losses[:, i * query_len : (i + 1) * query_len])
            weights = [
                (x / total - jnp.where(hit, 1.0, 0.0)) * inv_temp for hit, x in zip(hits, grown)
            ]
            for page in pages:
                row_weights[page].append(mine(weights[page]))
                row_lse[page].append(mine(smooth[page]))
            shares.append([[weights[page] * part for part in parts[page]] for page in pages])

        token_rows = block_of_tokens(tokens, b)
        for page in pages:
            count = integers[page : page + 1, :block_rows]
            live_count = count - slot * patch_local
            page_weight = jnp.concatenate(row_weights[page], axis=1)
            page_lse = jnp.concatenate(row_lse[page], axis=1) + smooth_tau * log_row(count)
            for start in range(0, patch_local, chunk):
                similar = contract(own[page, start : start + chunk], token_rows, 1, 1)
                coef = page_weight * jnp.exp2((similar - page_lse) * inv_tau_log2)
                coef = jnp.where(position < live_count - start, coef, 0.0).astype(jnp.bfloat16)
                grad = contract(coef, token_rows, 1, 0)
                if tokens.shape[0] > block_queries:
                    grad = grad + jnp.where(b == 0, 0.0, page_grad[page, start : start + chunk])
                page_grad[page, start : start + chunk] = grad

        def own_rows():
            row = lax.rem(group, block_queries) * query_len + slot * share
            picked = []
            for page in pages:
                for side in range(sides):
                    x = shares[0][page][side]
                    for other in range(1, halves):
                        x = jnp.where(row // lanes == other, shares[other][page][side], x)
                    picked.append(x)
            picked = jnp.concatenate(picked, axis=0)
            picked = pltpu.roll(picked, lax.rem(lanes - lax.rem(row, lanes), lanes), 1)
            columns = jnp.transpose(picked)[:share]
            grads = []
            for page in pages:
                for side in range(sides):
                    place = len(grads) * groups
                    first = sender(page, side) * lines + page % pair_pages * share
                    terms = [
                        columns[:, place + g : place + g + 1]
                        * heard[first + g * slots * lines : first + g * slots * lines + share]
                        for g in range(groups)
                    ]
                    grads.append(functools.reduce(jnp.add, terms))
            query_grad[0] = functools.reduce(jnp.add, grads)

        if tokens.shape[0] == block_queries:
            own_rows()
        else:
            pl.when(group // block_queries == b)(own_rows)

    over_blocks(tokens.shape[0] // block_queries, block)


def fetch_pairs(page_groups, slots, shifts):
    return [
        (group * slots + slot, (group ^ shifts[slot % 2]) * slots + slot)
        for group in range(page_groups)
        for slot in range(slots)
        if shifts[slot % 2]
    ]


def shards(page_groups, slots, query_tokens, page_patches, patch_counts, positive_page):
    query_local, query_len, width = query_tokens.shape
    page_local, patch_local, _ = page_patches.shape
    query_count = query_local * page_groups
    share = query_len // slots
    peers = page_groups * slots
    lines = page_local // 2 * (share + query_count * query_len // lanes)
    tile = math.gcd(lines, 8)
    smem = pl.BlockSpec(memory_space=pltpu.SMEM)
    vmem = pl.BlockSpec(memory_space=pltpu.VMEM)
    limit = (16 << 20) + 2 * peers * lines * lanes * 4
    params = pltpu.CompilerParams(vmem_limit_bytes=limit)

    partner = lax.ppermute(page_patches, "queries", [(i, i ^ 1) for i in range(slots)])
    token_shape = jax.ShapeDtypeStruct((page_groups, query_len, width), query_tokens.dtype)
    told_shape = jax.ShapeDtypeStruct((peers * lines, lanes), jnp.float32)
    scores = pltpu.VMEM((2, block_rows, patch_local), jnp.float32)
    small = pltpu.CompilerParams(vmem_limit_bytes=4 << 20)
    integer_shape = jax.ShapeDtypeStruct((page_local + 1, query_count * query_len), jnp.int32)
    if page_groups == 1 + sum(1 for side in fetches for shift in side if shift):
        fetched = [
            lax.ppermute(query_tokens, both, fetch_pairs(page_groups, slots, shifts))
            for shifts in zip(*fetches)
        ]
        held = pl.pallas_call(
            hold_kernel,
            out_shape=jax.ShapeDtypeStruct(page_patches.shape, page_patches.dtype),
            in_specs=[vmem],
            out_specs=vmem,
            compiler_params=small,
            cost_estimate=pl.CostEstimate(flops=0, bytes_accessed=1 << 24, transcendentals=0),
            name="hold",
        )(page_patches)
        gathered, mine, integers = pl.pallas_call(
            gather_kernel,
            out_shape=(
                jax.ShapeDtypeStruct((len(fetched), query_len, width), query_tokens.dtype),
                jax.ShapeDtypeStruct(query_tokens.shape, query_tokens.dtype),
                integer_shape,
            ),
            in_specs=[vmem] * (len(fetched) + 4),
            out_specs=(vmem, vmem, vmem),
            compiler_params=small,
            name="gather",
        )(patch_counts, positive_page, held, query_tokens, *fetched)
        others = lax.ppermute(gathered, "queries", [(i, i ^ 1) for i in range(slots)])
        told, tokens = pl.pallas_call(
            functools.partial(assembled_kernel, share, lines),
            out_shape=(told_shape, token_shape),
            in_specs=[vmem] * (5 + len(fetched)),
            out_specs=(vmem, vmem),
            scratch_shapes=[scores],
            compiler_params=params,
            name="forward",
        )(integers, held, partner, mine, *fetched, others)
    else:
        tokens = lax.all_to_all(
            jnp.broadcast_to(query_tokens, token_shape.shape), "pages", 0, 0, tiled=True
        )
        held = page_patches
        integers = pl.pallas_call(
            integer_rows,
            out_shape=integer_shape,
            in_specs=[vmem] * 2,
            out_specs=vmem,
            compiler_params=small,
            name="integers",
        )(patch_counts, positive_page)
        told = pl.pallas_call(
            functools.partial(forward_kernel, share, lines),
            out_shape=told_shape,
            in_specs=[vmem] * 4,
            out_specs=vmem,
            scratch_shapes=[scores],
            compiler_params=params,
            name="forward",
        )(integers, tokens, held, partner)
    told = told.reshape(peers, lines // tile, tile, lanes)
    heard = lax.all_to_all(told, both, 0, 0, tiled=True).reshape(peers * lines, lanes)
    return pl.pallas_call(
        functools.partial(backward_kernel, slots, share, lines),
        out_shape=(
            jax.ShapeDtypeStruct((query_count,), jnp.float32),
            jax.ShapeDtypeStruct((query_local, share, width), jnp.float32),
            jax.ShapeDtypeStruct((page_local, patch_local, width), jnp.float32),
        ),
        in_specs=[vmem] * 4,
        out_specs=(smem, vmem, vmem),
        compiler_params=params,
        name="backward",
    )(integers, heard, tokens, held)


def solution(mesh):
    in_specs = (P("pages", None, None), P("pages", "queries", None), P("pages"), P())
    out_specs = (P(), P("pages", "queries", None), P("pages", "queries", None))
    body = functools.partial(shards, mesh.shape["pages"], mesh.shape["queries"])
    return jax.shard_map(body, mesh=mesh, in_specs=in_specs, out_specs=out_specs, check_vma=False)
```

```python
import functools
import math

import jax
import jax.numpy as jnp
from jax import lax
from jax.experimental import pallas as pl
from jax.experimental.pallas import tpu as pltpu
from jax.sharding import PartitionSpec as P

smooth_tau = 0.05
page_temp = 0.02
neg_large = -1e30
inv_tau = 1.0 / smooth_tau
inv_temp = 1.0 / page_temp
inv_tau_log2 = inv_tau / math.log(2.0)
lanes = 128
block_rows = 256
both = ("pages", "queries")
fetches = ((6, 7, 2), (5, 1, 3, 4))


def contract(a, b, dim_a, dim_b):
    return lax.dot_general(
        a, b, (((dim_a,), (dim_b,)), ((), ())), preferred_element_type=jnp.float32
    )


def over_blocks(count, body):
    if count == 1:
        body(0)
    else:
        lax.fori_loop(0, count, lambda b, _: (body(b), 0)[1], 0)


def block_of_tokens(tokens, b):
    count = block_rows // tokens.shape[1]
    start = pl.multiple_of(b * count, count)
    return tokens[pl.ds(start, count)].reshape(block_rows, tokens.shape[2])


def log_row(count):
    return jnp.log(count.astype(jnp.float32))


def integer_rows(counts, positive, integers):
    counts, positive = counts[...][None], positive[...][None]
    page_local = counts.shape[1]
    rows = integers.shape[1]
    for page in range(page_local):
        integers[page : page + 1] = jnp.broadcast_to(counts[:, page : page + 1], (1, rows))
    query_count = positive.shape[1]
    row_query = lax.broadcasted_iota(jnp.int32, (1, rows), 1) // (rows // query_count)
    target = jnp.zeros((1, rows), jnp.int32)
    for query in range(query_count):
        target = jnp.where(row_query == query, positive[:, query : query + 1], target)
    integers[page_local : page_local + 1] = target


def hold_kernel(patches, out):
    out[...] = patches[...]


def gather_kernel(_, *refs):
    for i, ref in enumerate(refs[:-1]):
        refs[-1][i] = ref[0]


def pair_patches(own, partner):
    slot = lax.axis_index("queries")
    parity = lax.rem(slot, 2)
    patch_local = own.shape[1]
    sources = ((own, slot * patch_local), (partner, (slot + 1 - 2 * parity) * patch_local))
    return sources, parity, (slot - parity) * patch_local


def page_softmax(token_rows, sources, page, count, scores):
    rows = token_rows.shape[0]
    _, patch_local, width = sources[0][0].shape
    position = lax.broadcasted_iota(jnp.int32, (1, lanes), 1)
    places = [slice(start, start + lanes) for start in range(0, patch_local, lanes)]
    running = jnp.full((rows, lanes), neg_large, jnp.float32)
    for turn, (source, base) in enumerate(sources):
        similar = contract(token_rows, source[page], 1, 1)
        for place in places:
            live = jnp.broadcast_to(position < count - base - place.start, (rows, lanes))
            masked = jnp.where(live, similar[:, place], neg_large)
            scores[turn, :, place] = masked
            running = jnp.maximum(running, masked)
    highest = jnp.max(running, axis=1, keepdims=True)
    total = jnp.zeros((rows, lanes), jnp.float32)
    mean = jnp.zeros((rows, width), jnp.float32)
    for turn, (source, base) in enumerate(sources):
        coarse, fine = [], []
        for place in places:
            terms = jnp.exp2((scores[turn, :, place] - highest) * inv_tau_log2)
            total = total + terms
            coarse.append(terms.astype(jnp.bfloat16))
            fine.append((terms - coarse[-1].astype(jnp.float32)).astype(jnp.bfloat16))
        halves = [jnp.concatenate(part, axis=1) for part in (coarse, fine)]
        product = contract(jnp.concatenate(halves, axis=0), source[page], 1, 0)
        mean = mean + product[:rows] + product[rows:]
    total = jnp.sum(total, axis=1, keepdims=True)
    return mean * (1.0 / total), highest, total


def query_rows(columns, queries):
    query_len = columns[0].shape[0] // len(queries)
    per_row = lanes // query_len
    lane = lax.broadcasted_iota(jnp.int32, (query_len, lanes), 1)
    line = lax.broadcasted_iota(jnp.int32, (query_len, lanes), 0)
    masks = [lane == line + lax.rem(query, per_row) * query_len for query in queries]
    result = []
    for column in columns:
        rows = [jnp.zeros((1, lanes), jnp.float32) for _ in range(block_rows // lanes)]
        for i, (query, mask) in enumerate(zip(queries, masks)):
            part = jnp.where(mask, column[i * query_len : (i + 1) * query_len], 0.0)
            part = jnp.sum(part, axis=0, keepdims=True)
            rows = [
                row + jnp.where(query // per_row == half, part, 0.0)
                for half, row in enumerate(rows)
            ]
        result.append(jnp.concatenate(rows, axis=0))
    return result


def early_kernel(counts, positive, own, partner, mine, *refs):
    fetched, (means, lines, integers, scores) = refs[:-4], refs[-4:]
    integer_rows(counts, positive, integers)
    sources, parity, _ = pair_patches(own, partner)
    group = lax.axis_index("pages")
    count = integers[pl.ds(parity, 1), :block_rows][:, :lanes]
    blocks = [mine[0]] + [ref[0] for ref in fetched]
    queries = [group] + [
        group ^ jnp.where(parity == 0, first, second)
        for first, second in zip(*[side[: len(fetched)] for side in fetches])
    ]
    mean, highest, total = page_softmax(
        jnp.concatenate(blocks, axis=0), sources, parity, count, scores
    )
    means[...] = mean.reshape(means.shape)
    for i, rows in enumerate(query_rows((highest, total), queries)):
        lines[i] = rows


def late_kernel(
    share, integers, own, partner, early_means, early_lines, mine, *refs
):
    fetched, others, (out, tokens, scores) = refs[:-4], refs[-4], refs[-3:]
    sources, parity, first_slot = pair_patches(own, partner)
    group = lax.axis_index("pages")
    count = integers[pl.ds(parity, 1), :block_rows][:, :lanes]
    near = len(fetched) - 1
    blocks = [jnp.where(parity == 1, fetched[near][0], others[near])]
    blocks = blocks + [others[i] for i in range(near)]
    early_blocks = [mine[0]] + [ref[0] for ref in fetched[:near]]
    early_queries, queries = [group], [group ^ fetches[1][near]]
    for first, second in zip(*[side[:near] for side in fetches]):
        early_queries.append(group ^ jnp.where(parity == 0, first, second))
        queries.append(group ^ jnp.where(parity == 0, second, first))
    mean, highest, total = page_softmax(
        jnp.concatenate(blocks, axis=0), sources, parity, count, scores
    )
    query_len = blocks[0].shape[0]
    lines = out.shape[1] * share // query_len
    for i, query in enumerate(queries):
        tokens[pl.ds(query, 1)] = blocks[i][None]
        tokens[pl.ds(early_queries[i], 1)] = early_blocks[i][None]
        for k in range(query_len // share):
            part = mean[i * query_len + k * share : i * query_len + (k + 1) * share]
            place = (slice(k * lines, k * lines + share), slice(None))
            out[(pl.ds(query, 1), *place)] = part[None]
            part = early_means[i, k * share : (k + 1) * share]
            out[(pl.ds(early_queries[i], 1), *place)] = part[None]
    highest, total = query_rows((highest, total), queries)
    highest, total = highest + early_lines[0], total + early_lines[1]
    smooth = highest + smooth_tau * (jnp.log(total) - jnp.log(count.astype(jnp.float32)))
    smooth = jnp.where(count > first_slot, smooth, neg_large)
    peers = out.shape[0] * out.shape[1] // lines
    flat = out.reshape(peers * lines, lanes)
    for half in range(smooth.shape[0]):
        row = jnp.broadcast_to(smooth[half : half + 1], (peers, lanes))
        flat[pl.ds(share + half, peers, stride=lines)] = row


def forward_kernel(share, lines, integers, tokens, own, partner, out, scores):
    block_peers = block_rows // share
    peers = out.shape[0] // lines
    pair_pages = own.shape[0] // 2
    sources, parity, first_slot = pair_patches(own, partner)
    diagonal = lax.broadcasted_iota(jnp.int32, (lanes, lanes), 0) == lax.broadcasted_iota(
        jnp.int32, (lanes, lanes), 1
    )

    def as_row(column):
        return jnp.sum(jnp.where(diagonal, column, 0.0), axis=0, keepdims=True)

    def block(b):
        token_rows = block_of_tokens(tokens, b)
        for index in range(pair_pages):
            page = parity * pair_pages + index
            count = integers[pl.ds(page, 1), :block_rows][:, :lanes]
            mean, highest, total = page_softmax(token_rows, sources, page, count, scores)
            for i in range(block_peers):
                line = (b * block_peers + i) * lines + index * share
                out[pl.ds(line, share)] = mean[i * share : (i + 1) * share]
            log_count = jnp.log(count.astype(jnp.float32))
            for half in range(block_rows // lanes):
                rows = slice(half * lanes, (half + 1) * lanes)
                log_mean = jnp.log(as_row(total[rows])) - log_count
                smooth = as_row(highest[rows]) + smooth_tau * log_mean
                smooth = jnp.where(count > first_slot, smooth, neg_large)
                line = pair_pages * share + (b * pair_pages + index) * (block_rows // lanes) + half
                out[pl.ds(line, peers, stride=lines)] = jnp.broadcast_to(smooth, (peers, lanes))

    over_blocks(tokens.shape[0] * tokens.shape[1] // block_rows, block)


def backward_kernel(
    slots, share, lines, integers, heard, tokens, own, loss, query_grad, page_grad
):
    page_local, patch_local, width = own.shape
    query_len = tokens.shape[1]
    block_queries = block_rows // query_len
    halves = block_rows // lanes
    half_queries = lanes // query_len
    pair_pages = page_local // 2
    groups = heard.shape[0] // (lines * slots)
    sides = slots // 2
    slot = lax.axis_index("queries")
    group = lax.axis_index("pages")
    same_query = (
        lax.broadcasted_iota(jnp.int32, (lanes, lanes), 0) // query_len
        == lax.broadcasted_iota(jnp.int32, (lanes, lanes), 1) // query_len
    ).astype(jnp.bfloat16)
    group_ids = lax.broadcasted_iota(jnp.int32, (groups, lanes), 0)
    position = lax.broadcasted_iota(jnp.int32, (patch_local, block_rows), 0)
    pages = range(page_local)

    def sender(page, side):
        return 2 * side + page // pair_pages

    def token_sums(x):
        coarse = x.astype(jnp.bfloat16)
        rest = x - coarse.astype(jnp.float32)
        middle = rest.astype(jnp.bfloat16)
        fine = (rest - middle.astype(jnp.float32)).astype(jnp.bfloat16)
        sums = contract(jnp.concatenate([coarse, middle, fine], axis=0), same_query, 1, 0)
        size = x.shape[0]
        return sums[:size] + sums[size : 2 * size] + sums[2 * size :]

    def mine(x):
        return jnp.sum(jnp.where(group_ids == group, x, 0.0), axis=0, keepdims=True)

    def block(b):
        row_weights = [[] for _ in pages]
        row_lse = [[] for _ in pages]
        shares = []
        for half in range(halves):
            smooth = []
            parts = []
            for page in pages:
                line = pair_pages * share + (b * pair_pages + page % pair_pages) * halves + half
                heights = [
                    heard[pl.ds(sender(page, side) * lines + line, groups, stride=slots * lines)]
                    for side in range(sides)
                ]
                highest = functools.reduce(jnp.maximum, heights)
                terms = [jnp.exp2((x - highest) * inv_tau_log2) for x in heights]
                total = functools.reduce(jnp.add, terms)
                smooth.append(highest + smooth_tau * jnp.log(total))
                parts.append([x / total for x in terms])
            sums = token_sums(jnp.concatenate(smooth, axis=0)) * inv_temp
            logits = [sums[page * groups : (page + 1) * groups] for page in pages]
            top = functools.reduce(jnp.maximum, logits)
            top = jnp.max(top, axis=0, keepdims=True)
            grown = [jnp.exp(x - top) for x in logits]
            total = jnp.sum(functools.reduce(jnp.add, grown), axis=0, keepdims=True)
            first_query = b * block_queries + half * half_queries
            line = pl.multiple_of(first_query * query_len, lanes)
            target = integers[page_local : page_local + 1, pl.ds(line, lanes)]
            hits = [group_ids * page_local + page == target for page in pages]
            found = functools.reduce(
                jnp.add, [jnp.where(hit, x, 0.0) for hit, x in zip(hits, logits)]
            )
            losses = top + jnp.log(total) - jnp.sum(found, axis=0, keepdims=True)
            for i in range(half_queries):
                loss[first_query + i] = jnp.max(losses[:, i * query_len : (i + 1) * query_len])
            weights = [
                (x / total - jnp.where(hit, 1.0, 0.0)) * inv_temp for hit, x in zip(hits, grown)
            ]
            for page in pages:
                row_weights[page].append(mine(weights[page]))
                row_lse[page].append(mine(smooth[page]))
            shares.append([[weights[page] * part for part in parts[page]] for page in pages])

        token_rows = block_of_tokens(tokens, b)
        for page in pages:
            count = integers[page : page + 1, :block_rows]
            live_count = count - slot * patch_local
            page_weight = jnp.concatenate(row_weights[page], axis=1)
            page_lse = jnp.concatenate(row_lse[page], axis=1) + smooth_tau * log_row(count)
            similar = contract(own[page], token_rows, 1, 1)
            coef = page_weight * jnp.exp2((similar - page_lse) * inv_tau_log2)
            coef = jnp.where(position < live_count, coef, 0.0).astype(jnp.bfloat16)
            grad = contract(coef, token_rows, 1, 0)
            if tokens.shape[0] > block_queries:
                grad = grad + jnp.where(b == 0, 0.0, page_grad[page])
            page_grad[page] = grad

        def own_rows():
            row = lax.rem(group, block_queries) * query_len + slot * share
            picked = []
            for page in pages:
                for side in range(sides):
                    x = shares[0][page][side]
                    for other in range(1, halves):
                        x = jnp.where(row // lanes == other, shares[other][page][side], x)
                    picked.append(x)
            picked = jnp.concatenate(picked, axis=0)
            picked = pltpu.roll(picked, lax.rem(lanes - lax.rem(row, lanes), lanes), 1)
            columns = jnp.transpose(picked)[:share]
            grads = []
            for page in pages:
                for side in range(sides):
                    place = len(grads) * groups
                    first = sender(page, side) * lines + page % pair_pages * share
                    terms = [
                        columns[:, place + g : place + g + 1]
                        * heard[first + g * slots * lines : first + g * slots * lines + share]
                        for g in range(groups)
                    ]
                    grads.append(functools.reduce(jnp.add, terms))
            query_grad[0] = functools.reduce(jnp.add, grads)

        if tokens.shape[0] == block_queries:
            own_rows()
        else:
            pl.when(group // block_queries == b)(own_rows)

    over_blocks(tokens.shape[0] // block_queries, block)


def fetch_pairs(page_groups, slots, index):
    return [
        (group * slots + slot, (group ^ shift) * slots + slot)
        for slot in range(slots)
        for shift in fetches[slot % 2][index : index + 1]
        for group in range(page_groups)
    ]


def shards(page_groups, slots, query_tokens, page_patches, patch_counts, positive_page):
    query_local, query_len, width = query_tokens.shape
    page_local, patch_local, _ = page_patches.shape
    query_count = query_local * page_groups
    share = query_len // slots
    peers = page_groups * slots
    lines = page_local // 2 * (share + query_count * query_len // lanes)
    tile = math.gcd(lines, 8)
    smem = pl.BlockSpec(memory_space=pltpu.SMEM)
    vmem = pl.BlockSpec(memory_space=pltpu.VMEM)
    limit = (16 << 20) + 2 * peers * lines * lanes * 4
    params = pltpu.CompilerParams(vmem_limit_bytes=limit)

    partner = lax.ppermute(page_patches, "queries", [(i, i ^ 1) for i in range(slots)])
    token_shape = jax.ShapeDtypeStruct((page_groups, query_len, width), query_tokens.dtype)
    told_shape = jax.ShapeDtypeStruct((peers * lines, lanes), jnp.float32)
    scores = pltpu.VMEM((2, block_rows, patch_local), jnp.float32)
    small = pltpu.CompilerParams(vmem_limit_bytes=4 << 20)
    integer_shape = jax.ShapeDtypeStruct((page_local + 1, query_count * query_len), jnp.int32)
    if page_local == 2 and page_groups == 1 + sum(len(side) for side in fetches):
        fetched = [
            lax.ppermute(query_tokens, both, fetch_pairs(page_groups, slots, i))
            for i in range(len(fetches[1]))
        ]
        held = pl.pallas_call(
            hold_kernel,
            out_shape=jax.ShapeDtypeStruct(page_patches.shape, page_patches.dtype),
            in_specs=[vmem],
            out_specs=vmem,
            compiler_params=small,
            cost_estimate=pl.CostEstimate(flops=0, bytes_accessed=1 << 24, transcendentals=0),
            name="hold",
        )(page_patches)
        gathered = pl.pallas_call(
            gather_kernel,
            out_shape=jax.ShapeDtypeStruct((len(fetched), query_len, width), query_tokens.dtype),
            in_specs=[vmem] * (len(fetched) + 1),
            out_specs=vmem,
            compiler_params=small,
            name="gather",
        )(held, *fetched)
        others = lax.ppermute(gathered, "queries", [(i, i ^ 1) for i in range(slots)])
        near = len(fetched) - 1
        half_scores = pltpu.VMEM((2, block_rows // 2, patch_local), jnp.float32)
        means, rows, integers = pl.pallas_call(
            early_kernel,
            out_shape=(
                jax.ShapeDtypeStruct((near + 1, query_len, width), jnp.float32),
                jax.ShapeDtypeStruct((2, block_rows // lanes, lanes), jnp.float32),
                integer_shape,
            ),
            in_specs=[vmem] * (5 + near),
            out_specs=(vmem, vmem, vmem),
            scratch_shapes=[half_scores],
            compiler_params=params,
            cost_estimate=pl.CostEstimate(flops=0, bytes_accessed=1 << 24, transcendentals=0),
            name="early",
        )(patch_counts, positive_page, held, partner, query_tokens, *fetched[:near])
        told, tokens = pl.pallas_call(
            functools.partial(late_kernel, share),
            out_shape=(
                jax.ShapeDtypeStruct((page_groups, slots * lines, lanes), jnp.float32),
                token_shape,
            ),
            in_specs=[vmem] * (7 + len(fetched)),
            out_specs=(vmem, vmem),
            scratch_shapes=[half_scores],
            compiler_params=params,
            name="late",
        )(integers, held, partner, means, rows, query_tokens, *fetched, others)
    else:
        tokens = lax.all_to_all(
            jnp.broadcast_to(query_tokens, token_shape.shape), "pages", 0, 0, tiled=True
        )
        held = page_patches
        integers = pl.pallas_call(
            integer_rows,
            out_shape=integer_shape,
            in_specs=[vmem] * 2,
            out_specs=vmem,
            compiler_params=small,
            name="integers",
        )(patch_counts, positive_page)
        told = pl.pallas_call(
            functools.partial(forward_kernel, share, lines),
            out_shape=told_shape,
            in_specs=[vmem] * 4,
            out_specs=vmem,
            scratch_shapes=[scores],
            compiler_params=params,
            name="forward",
        )(integers, tokens, held, partner)
    told = told.reshape(peers, lines // tile, tile, lanes)
    heard = lax.all_to_all(told, both, 0, 0, tiled=True).reshape(peers * lines, lanes)
    return pl.pallas_call(
        functools.partial(backward_kernel, slots, share, lines),
        out_shape=(
            jax.ShapeDtypeStruct((query_count,), jnp.float32),
            jax.ShapeDtypeStruct((query_local, share, width), jnp.float32),
            jax.ShapeDtypeStruct((page_local, patch_local, width), jnp.float32),
        ),
        in_specs=[vmem] * 4,
        out_specs=(smem, vmem, vmem),
        compiler_params=params,
        name="backward",
    )(integers, heard, tokens, held)


def solution(mesh):
    in_specs = (P("pages", None, None), P("pages", "queries", None), P("pages"), P())
    out_specs = (P(), P("pages", "queries", None), P("pages", "queries", None))
    body = functools.partial(shards, mesh.shape["pages"], mesh.shape["queries"])
    return jax.shard_map(body, mesh=mesh, in_specs=in_specs, out_specs=out_specs, check_vma=False)
```

```python
import functools
import math

import jax
import jax.numpy as jnp
from jax import lax
from jax.experimental import pallas as pl
from jax.experimental.pallas import tpu as pltpu
from jax.sharding import PartitionSpec as P

smooth_tau = 0.05
page_temp = 0.02
neg_large = -1e30
inv_tau = 1.0 / smooth_tau
inv_temp = 1.0 / page_temp
inv_tau_log2 = inv_tau / math.log(2.0)
lanes = 128
block_rows = 256
both = ("pages", "queries")
fetches = ((6, 2, 7), (3, 5, 1, 4))


def contract(a, b, dim_a, dim_b):
    return lax.dot_general(
        a, b, (((dim_a,), (dim_b,)), ((), ())), preferred_element_type=jnp.float32
    )


def over_blocks(count, body):
    if count == 1:
        body(0)
    else:
        lax.fori_loop(0, count, lambda b, _: (body(b), 0)[1], 0)


def block_of_tokens(tokens, b):
    count = block_rows // tokens.shape[1]
    start = pl.multiple_of(b * count, count)
    return tokens[pl.ds(start, count)].reshape(block_rows, tokens.shape[2])


def log_row(count):
    return jnp.log(count.astype(jnp.float32))


def integer_rows(counts, positive, integers):
    counts, positive = counts[...][None], positive[...][None]
    page_local = counts.shape[1]
    rows = integers.shape[1]
    for page in range(page_local):
        integers[page : page + 1] = jnp.broadcast_to(counts[:, page : page + 1], (1, rows))
    query_count = positive.shape[1]
    row_query = lax.broadcasted_iota(jnp.int32, (1, rows), 1) // (rows // query_count)
    target = jnp.zeros((1, rows), jnp.int32)
    for query in range(query_count):
        target = jnp.where(row_query == query, positive[:, query : query + 1], target)
    integers[page_local : page_local + 1] = target


def hold_kernel(patches, out):
    out[...] = patches[...]


def gather_kernel(_, *refs):
    for i, ref in enumerate(refs[:-1]):
        refs[-1][i] = ref[0]


def pair_patches(own, partner):
    slot = lax.axis_index("queries")
    parity = lax.rem(slot, 2)
    patch_local = own.shape[1]
    sources = ((own, slot * patch_local), (partner, (slot + 1 - 2 * parity) * patch_local))
    return sources, parity, (slot - parity) * patch_local


def page_softmax(token_rows, sources, page, count, scores):
    rows = token_rows.shape[0]
    _, patch_local, width = sources[0][0].shape
    position = lax.broadcasted_iota(jnp.int32, (1, lanes), 1)
    places = [slice(start, start + lanes) for start in range(0, patch_local, lanes)]
    running = jnp.full((rows, lanes), neg_large, jnp.float32)
    for turn, (source, base) in enumerate(sources):
        similar = contract(token_rows, source[page], 1, 1)
        for place in places:
            live = jnp.broadcast_to(position < count - base - place.start, (rows, lanes))
            masked = jnp.where(live, similar[:, place], neg_large)
            scores[turn, :, place] = masked
            running = jnp.maximum(running, masked)
    highest = jnp.max(running, axis=1, keepdims=True)
    total = jnp.zeros((rows, lanes), jnp.float32)
    mean = jnp.zeros((rows, width), jnp.float32)
    for turn, (source, base) in enumerate(sources):
        coarse, fine = [], []
        for place in places:
            terms = jnp.exp2((scores[turn, :, place] - highest) * inv_tau_log2)
            total = total + terms
            coarse.append(terms.astype(jnp.bfloat16))
            fine.append((terms - coarse[-1].astype(jnp.float32)).astype(jnp.bfloat16))
        halves = [jnp.concatenate(part, axis=1) for part in (coarse, fine)]
        product = contract(jnp.concatenate(halves, axis=0), source[page], 1, 0)
        mean = mean + product[:rows] + product[rows:]
    total = jnp.sum(total, axis=1, keepdims=True)
    return mean * (1.0 / total), highest, total


def query_rows(columns, queries):
    query_len = columns[0].shape[0] // len(queries)
    per_row = lanes // query_len
    lane = lax.broadcasted_iota(jnp.int32, (query_len, lanes), 1)
    line = lax.broadcasted_iota(jnp.int32, (query_len, lanes), 0)
    masks = [lane == line + lax.rem(query, per_row) * query_len for query in queries]
    result = []
    for column in columns:
        rows = [jnp.zeros((1, lanes), jnp.float32) for _ in range(block_rows // lanes)]
        for i, (query, mask) in enumerate(zip(queries, masks)):
            part = jnp.where(mask, column[i * query_len : (i + 1) * query_len], 0.0)
            part = jnp.sum(part, axis=0, keepdims=True)
            rows = [
                row + jnp.where(query // per_row == half, part, 0.0)
                for half, row in enumerate(rows)
            ]
        result.append(jnp.concatenate(rows, axis=0))
    return result


def early_kernel(counts, positive, own, partner, mine, *refs):
    fetched, (means, lines, integers, scores) = refs[:-4], refs[-4:]
    integer_rows(counts, positive, integers)
    sources, parity, _ = pair_patches(own, partner)
    group = lax.axis_index("pages")
    count = integers[pl.ds(parity, 1), :block_rows][:, :lanes]
    blocks = [mine[0]] + [ref[0] for ref in fetched]
    queries = [group] + [
        group ^ jnp.where(parity == 0, first, second)
        for first, second in zip(*[side[: len(fetched)] for side in fetches])
    ]
    mean, highest, total = page_softmax(
        jnp.concatenate(blocks, axis=0), sources, parity, count, scores
    )
    means[...] = mean.reshape(means.shape)
    for i, rows in enumerate(query_rows((highest, total), queries)):
        lines[i] = rows


def late_kernel(
    share, integers, own, partner, early_means, early_lines, mine, *refs
):
    fetched, others, (out, tokens, scores) = refs[:-4], refs[-4], refs[-3:]
    sources, parity, first_slot = pair_patches(own, partner)
    group = lax.axis_index("pages")
    count = integers[pl.ds(parity, 1), :block_rows][:, :lanes]
    near = len(fetched) - 1
    blocks = [jnp.where(parity == 1, fetched[near][0], others[near])]
    blocks = blocks + [others[i] for i in range(near)]
    early_blocks = [mine[0]] + [ref[0] for ref in fetched[:near]]
    early_queries, queries = [group], [group ^ fetches[1][near]]
    for first, second in zip(*[side[:near] for side in fetches]):
        early_queries.append(group ^ jnp.where(parity == 0, first, second))
        queries.append(group ^ jnp.where(parity == 0, second, first))
    mean, highest, total = page_softmax(
        jnp.concatenate(blocks, axis=0), sources, parity, count, scores
    )
    query_len = blocks[0].shape[0]
    lines = out.shape[1] * share // query_len
    for i, query in enumerate(queries):
        tokens[pl.ds(query, 1)] = blocks[i][None]
        tokens[pl.ds(early_queries[i], 1)] = early_blocks[i][None]
        for k in range(query_len // share):
            part = mean[i * query_len + k * share : i * query_len + (k + 1) * share]
            place = (slice(k * lines, k * lines + share), slice(None))
            out[(pl.ds(query, 1), *place)] = part[None]
            part = early_means[i, k * share : (k + 1) * share]
            out[(pl.ds(early_queries[i], 1), *place)] = part[None]
    highest, total = query_rows((highest, total), queries)
    highest, total = highest + early_lines[0], total + early_lines[1]
    smooth = highest + smooth_tau * (jnp.log(total) - jnp.log(count.astype(jnp.float32)))
    smooth = jnp.where(count > first_slot, smooth, neg_large)
    for half in range(smooth.shape[0]):
        row = jnp.broadcast_to(smooth[half : half + 1][None], (out.shape[0], 1, lanes))
        for k in range(query_len // share):
            line = k * lines + share + half
            out[:, line : line + 1] = row


def forward_kernel(share, lines, integers, tokens, own, partner, out, scores):
    block_peers = block_rows // share
    peers = out.shape[0] // lines
    pair_pages = own.shape[0] // 2
    sources, parity, first_slot = pair_patches(own, partner)
    diagonal = lax.broadcasted_iota(jnp.int32, (lanes, lanes), 0) == lax.broadcasted_iota(
        jnp.int32, (lanes, lanes), 1
    )

    def as_row(column):
        return jnp.sum(jnp.where(diagonal, column, 0.0), axis=0, keepdims=True)

    def block(b):
        token_rows = block_of_tokens(tokens, b)
        for index in range(pair_pages):
            page = parity * pair_pages + index
            count = integers[pl.ds(page, 1), :block_rows][:, :lanes]
            mean, highest, total = page_softmax(token_rows, sources, page, count, scores)
            for i in range(block_peers):
                line = (b * block_peers + i) * lines + index * share
                out[pl.ds(line, share)] = mean[i * share : (i + 1) * share]
            log_count = jnp.log(count.astype(jnp.float32))
            for half in range(block_rows // lanes):
                rows = slice(half * lanes, (half + 1) * lanes)
                log_mean = jnp.log(as_row(total[rows])) - log_count
                smooth = as_row(highest[rows]) + smooth_tau * log_mean
                smooth = jnp.where(count > first_slot, smooth, neg_large)
                line = pair_pages * share + (b * pair_pages + index) * (block_rows // lanes) + half
                out[pl.ds(line, peers, stride=lines)] = jnp.broadcast_to(smooth, (peers, lanes))

    over_blocks(tokens.shape[0] * tokens.shape[1] // block_rows, block)


def backward_kernel(
    slots, share, lines, integers, heard, tokens, own, loss, query_grad, page_grad
):
    page_local, patch_local, width = own.shape
    query_len = tokens.shape[1]
    block_queries = block_rows // query_len
    halves = block_rows // lanes
    half_queries = lanes // query_len
    pair_pages = page_local // 2
    groups = heard.shape[0] // (lines * slots)
    sides = slots // 2
    slot = lax.axis_index("queries")
    group = lax.axis_index("pages")
    same_query = (
        lax.broadcasted_iota(jnp.int32, (lanes, lanes), 0) // query_len
        == lax.broadcasted_iota(jnp.int32, (lanes, lanes), 1) // query_len
    ).astype(jnp.bfloat16)
    group_ids = lax.broadcasted_iota(jnp.int32, (groups, lanes), 0)
    position = lax.broadcasted_iota(jnp.int32, (patch_local, block_rows), 0)
    pages = range(page_local)

    def sender(page, side):
        return 2 * side + page // pair_pages

    def token_sums(x):
        coarse = x.astype(jnp.bfloat16)
        rest = x - coarse.astype(jnp.float32)
        middle = rest.astype(jnp.bfloat16)
        fine = (rest - middle.astype(jnp.float32)).astype(jnp.bfloat16)
        sums = contract(jnp.concatenate([coarse, middle, fine], axis=0), same_query, 1, 0)
        size = x.shape[0]
        return sums[:size] + sums[size : 2 * size] + sums[2 * size :]

    def mine(x):
        return jnp.sum(jnp.where(group_ids == group, x, 0.0), axis=0, keepdims=True)

    def block(b):
        row_weights = [[] for _ in pages]
        row_lse = [[] for _ in pages]
        shares = []
        for half in range(halves):
            smooth = []
            parts = []
            for page in pages:
                line = pair_pages * share + (b * pair_pages + page % pair_pages) * halves + half
                heights = [
                    heard[pl.ds(sender(page, side) * lines + line, groups, stride=slots * lines)]
                    for side in range(sides)
                ]
                highest = functools.reduce(jnp.maximum, heights)
                terms = [jnp.exp2((x - highest) * inv_tau_log2) for x in heights]
                total = functools.reduce(jnp.add, terms)
                smooth.append(highest + smooth_tau * jnp.log(total))
                parts.append([x / total for x in terms])
            sums = token_sums(jnp.concatenate(smooth, axis=0)) * inv_temp
            logits = [sums[page * groups : (page + 1) * groups] for page in pages]
            top = functools.reduce(jnp.maximum, logits)
            top = jnp.max(top, axis=0, keepdims=True)
            grown = [jnp.exp(x - top) for x in logits]
            total = jnp.sum(functools.reduce(jnp.add, grown), axis=0, keepdims=True)
            first_query = b * block_queries + half * half_queries
            line = pl.multiple_of(first_query * query_len, lanes)
            target = integers[page_local : page_local + 1, pl.ds(line, lanes)]
            hits = [group_ids * page_local + page == target for page in pages]
            found = functools.reduce(
                jnp.add, [jnp.where(hit, x, 0.0) for hit, x in zip(hits, logits)]
            )
            losses = top + jnp.log(total) - jnp.sum(found, axis=0, keepdims=True)
            for i in range(half_queries):
                loss[first_query + i] = jnp.max(losses[:, i * query_len : (i + 1) * query_len])
            weights = [
                (x / total - jnp.where(hit, 1.0, 0.0)) * inv_temp for hit, x in zip(hits, grown)
            ]
            for page in pages:
                row_weights[page].append(mine(weights[page]))
                row_lse[page].append(mine(smooth[page]))
            shares.append([[weights[page] * part for part in parts[page]] for page in pages])

        token_rows = block_of_tokens(tokens, b)
        for page in pages:
            count = integers[page : page + 1, :block_rows]
            live_count = count - slot * patch_local
            page_weight = jnp.concatenate(row_weights[page], axis=1)
            page_lse = jnp.concatenate(row_lse[page], axis=1) + smooth_tau * log_row(count)
            similar = contract(own[page], token_rows, 1, 1)
            coef = page_weight * jnp.exp2((similar - page_lse) * inv_tau_log2)
            coef = jnp.where(position < live_count, coef, 0.0).astype(jnp.bfloat16)
            grad = contract(coef, token_rows, 1, 0)
            if tokens.shape[0] > block_queries:
                grad = grad + jnp.where(b == 0, 0.0, page_grad[page])
            page_grad[page] = grad

        def own_rows():
            row = lax.rem(group, block_queries) * query_len + slot * share
            picked = []
            for page in pages:
                for side in range(sides):
                    x = shares[0][page][side]
                    for other in range(1, halves):
                        x = jnp.where(row // lanes == other, shares[other][page][side], x)
                    picked.append(x)
            picked = jnp.concatenate(picked, axis=0)
            picked = pltpu.roll(picked, lax.rem(lanes - lax.rem(row, lanes), lanes), 1)
            columns = jnp.transpose(picked)[:share]
            grads = []
            for page in pages:
                for side in range(sides):
                    place = len(grads) * groups
                    first = sender(page, side) * lines + page % pair_pages * share
                    terms = [
                        columns[:, place + g : place + g + 1]
                        * heard[first + g * slots * lines : first + g * slots * lines + share]
                        for g in range(groups)
                    ]
                    grads.append(functools.reduce(jnp.add, terms))
            query_grad[0] = functools.reduce(jnp.add, grads)

        if tokens.shape[0] == block_queries:
            own_rows()
        else:
            pl.when(group // block_queries == b)(own_rows)

    over_blocks(tokens.shape[0] // block_queries, block)


def fetch_pairs(page_groups, slots, index):
    return [
        (group * slots + slot, (group ^ shift) * slots + slot)
        for slot in range(slots)
        for shift in (fetches[slot % 2] + (0,))[index : index + 1]
        for group in range(page_groups)
    ]


def shards(page_groups, slots, query_tokens, page_patches, patch_counts, positive_page):
    query_local, query_len, width = query_tokens.shape
    page_local, patch_local, _ = page_patches.shape
    query_count = query_local * page_groups
    share = query_len // slots
    peers = page_groups * slots
    lines = page_local // 2 * (share + query_count * query_len // lanes)
    tile = math.gcd(lines, 8)
    smem = pl.BlockSpec(memory_space=pltpu.SMEM)
    vmem = pl.BlockSpec(memory_space=pltpu.VMEM)
    limit = (16 << 20) + 2 * peers * lines * lanes * 4
    params = pltpu.CompilerParams(vmem_limit_bytes=limit)

    partner = lax.ppermute(page_patches, "queries", [(i, i ^ 1) for i in range(slots)])
    token_shape = jax.ShapeDtypeStruct((page_groups, query_len, width), query_tokens.dtype)
    told_shape = jax.ShapeDtypeStruct((peers * lines, lanes), jnp.float32)
    scores = pltpu.VMEM((2, block_rows, patch_local), jnp.float32)
    small = pltpu.CompilerParams(vmem_limit_bytes=4 << 20)
    integer_shape = jax.ShapeDtypeStruct((page_local + 1, query_count * query_len), jnp.int32)
    if page_local == 2 and page_groups == 1 + sum(len(side) for side in fetches):
        fetched = [
            lax.ppermute(query_tokens, both, fetch_pairs(page_groups, slots, i))
            for i in range(len(fetches[1]))
        ]
        held = pl.pallas_call(
            hold_kernel,
            out_shape=jax.ShapeDtypeStruct(page_patches.shape, page_patches.dtype),
            in_specs=[vmem],
            out_specs=vmem,
            compiler_params=small,
            name="hold",
        )(page_patches)
        gathered = pl.pallas_call(
            gather_kernel,
            out_shape=jax.ShapeDtypeStruct((len(fetched), query_len, width), query_tokens.dtype),
            in_specs=[vmem] * (len(fetched) + 1),
            out_specs=vmem,
            compiler_params=small,
            name="gather",
        )(held, *fetched)
        others = lax.ppermute(gathered, "queries", [(i, i ^ 1) for i in range(slots)])
        near = len(fetched) - 1
        half_scores = pltpu.VMEM((2, block_rows // 2, patch_local), jnp.float32)
        means, rows, integers = pl.pallas_call(
            early_kernel,
            out_shape=(
                jax.ShapeDtypeStruct((near + 1, query_len, width), jnp.float32),
                jax.ShapeDtypeStruct((2, block_rows // lanes, lanes), jnp.float32),
                integer_shape,
            ),
            in_specs=[vmem] * (5 + near),
            out_specs=(vmem, vmem, vmem),
            scratch_shapes=[half_scores],
            compiler_params=params,
            name="early",
        )(patch_counts, positive_page, held, partner, query_tokens, *fetched[:near])
        told, tokens = pl.pallas_call(
            functools.partial(late_kernel, share),
            out_shape=(
                jax.ShapeDtypeStruct((page_groups, slots * lines, lanes), jnp.float32),
                token_shape,
            ),
            in_specs=[vmem] * (7 + len(fetched)),
            out_specs=(vmem, vmem),
            scratch_shapes=[half_scores],
            compiler_params=params,
            name="late",
        )(integers, held, partner, means, rows, query_tokens, *fetched, others)
    else:
        tokens = lax.all_to_all(
            jnp.broadcast_to(query_tokens, token_shape.shape), "pages", 0, 0, tiled=True
        )
        held = page_patches
        integers = pl.pallas_call(
            integer_rows,
            out_shape=integer_shape,
            in_specs=[vmem] * 2,
            out_specs=vmem,
            compiler_params=small,
            name="integers",
        )(patch_counts, positive_page)
        told = pl.pallas_call(
            functools.partial(forward_kernel, share, lines),
            out_shape=told_shape,
            in_specs=[vmem] * 4,
            out_specs=vmem,
            scratch_shapes=[scores],
            compiler_params=params,
            name="forward",
        )(integers, tokens, held, partner)
    told = told.reshape(peers, lines // tile, tile, lanes)
    heard = lax.all_to_all(told, both, 0, 0, tiled=True).reshape(peers * lines, lanes)
    return pl.pallas_call(
        functools.partial(backward_kernel, slots, share, lines),
        out_shape=(
            jax.ShapeDtypeStruct((query_count,), jnp.float32),
            jax.ShapeDtypeStruct((query_local, share, width), jnp.float32),
            jax.ShapeDtypeStruct((page_local, patch_local, width), jnp.float32),
        ),
        in_specs=[vmem] * 4,
        out_specs=(smem, vmem, vmem),
        compiler_params=params,
        name="backward",
    )(integers, heard, tokens, held)


def solution(mesh):
    in_specs = (P("pages", None, None), P("pages", "queries", None), P("pages"), P())
    out_specs = (P(), P("pages", "queries", None), P("pages", "queries", None))
    body = functools.partial(shards, mesh.shape["pages"], mesh.shape["queries"])
    return jax.shard_map(body, mesh=mesh, in_specs=in_specs, out_specs=out_specs, check_vma=False)
```

```python
import functools
import math

import jax
import jax.numpy as jnp
from jax import lax
from jax.experimental import pallas as pl
from jax.experimental.pallas import tpu as pltpu
from jax.sharding import PartitionSpec as P

smooth_tau = 0.05
page_temp = 0.02
neg_large = -1e30
inv_tau = 1.0 / smooth_tau
inv_temp = 1.0 / page_temp
inv_tau_log2 = inv_tau / math.log(2.0)
lanes = 128
block_rows = 256
both = ("pages", "queries")
fetches = ((6, 2, 7), (3, 5, 1, 4))


def contract(a, b, dim_a, dim_b):
    return lax.dot_general(
        a, b, (((dim_a,), (dim_b,)), ((), ())), preferred_element_type=jnp.float32
    )


def over_blocks(count, body):
    if count == 1:
        body(0)
    else:
        lax.fori_loop(0, count, lambda b, _: (body(b), 0)[1], 0)


def block_of_tokens(tokens, b):
    count = block_rows // tokens.shape[1]
    start = pl.multiple_of(b * count, count)
    return tokens[pl.ds(start, count)].reshape(block_rows, tokens.shape[2])


def log_row(count):
    return jnp.log(count.astype(jnp.float32))


def integer_rows(counts, positive, integers):
    counts, positive = counts[...][None], positive[...][None]
    page_local = counts.shape[1]
    rows = integers.shape[1]
    for page in range(page_local):
        integers[page : page + 1] = jnp.broadcast_to(counts[:, page : page + 1], (1, rows))
    query_count = positive.shape[1]
    row_query = lax.broadcasted_iota(jnp.int32, (1, rows), 1) // (rows // query_count)
    target = jnp.zeros((1, rows), jnp.int32)
    for query in range(query_count):
        target = jnp.where(row_query == query, positive[:, query : query + 1], target)
    integers[page_local : page_local + 1] = target


def hold_kernel(patches, out):
    out[...] = patches[...]


def gather_kernel(_, *refs):
    for i, ref in enumerate(refs[:-1]):
        refs[-1][i] = ref[0]


def pair_patches(own, partner):
    slot = lax.axis_index("queries")
    parity = lax.rem(slot, 2)
    patch_local = own.shape[1]
    sources = ((own, slot * patch_local), (partner, (slot + 1 - 2 * parity) * patch_local))
    return sources, parity, (slot - parity) * patch_local


def page_softmax(token_rows, sources, page, count, scores):
    rows = token_rows.shape[0]
    _, patch_local, width = sources[0][0].shape
    position = lax.broadcasted_iota(jnp.int32, (1, lanes), 1)
    places = [slice(start, start + lanes) for start in range(0, patch_local, lanes)]
    running = jnp.full((rows, lanes), neg_large, jnp.float32)
    for turn, (source, base) in enumerate(sources):
        similar = contract(token_rows, source[page], 1, 1)
        for place in places:
            live = jnp.broadcast_to(position < count - base - place.start, (rows, lanes))
            masked = jnp.where(live, similar[:, place], neg_large)
            scores[turn, :, place] = masked
            running = jnp.maximum(running, masked)
    highest = jnp.max(running, axis=1, keepdims=True)
    total = jnp.zeros((rows, lanes), jnp.float32)
    mean = jnp.zeros((rows, width), jnp.float32)
    for turn, (source, base) in enumerate(sources):
        coarse, fine = [], []
        for place in places:
            terms = jnp.exp2((scores[turn, :, place] - highest) * inv_tau_log2)
            total = total + terms
            coarse.append(terms.astype(jnp.bfloat16))
            fine.append((terms - coarse[-1].astype(jnp.float32)).astype(jnp.bfloat16))
        halves = [jnp.concatenate(part, axis=1) for part in (coarse, fine)]
        product = contract(jnp.concatenate(halves, axis=0), source[page], 1, 0)
        mean = mean + product[:rows] + product[rows:]
    total = jnp.sum(total, axis=1, keepdims=True)
    return mean * (1.0 / total), highest, total


def query_rows(columns, queries):
    query_len = columns[0].shape[0] // len(queries)
    per_row = lanes // query_len
    lane = lax.broadcasted_iota(jnp.int32, (query_len, lanes), 1)
    line = lax.broadcasted_iota(jnp.int32, (query_len, lanes), 0)
    masks = [lane == line + lax.rem(query, per_row) * query_len for query in queries]
    result = []
    for column in columns:
        rows = [jnp.zeros((1, lanes), jnp.float32) for _ in range(block_rows // lanes)]
        for i, (query, mask) in enumerate(zip(queries, masks)):
            part = jnp.where(mask, column[i * query_len : (i + 1) * query_len], 0.0)
            part = jnp.sum(part, axis=0, keepdims=True)
            rows = [
                row + jnp.where(query // per_row == half, part, 0.0)
                for half, row in enumerate(rows)
            ]
        result.append(jnp.concatenate(rows, axis=0))
    return result


def early_kernel(counts, positive, own, partner, mine, *refs):
    fetched, (means, lines, integers, scores) = refs[:-4], refs[-4:]
    integer_rows(counts, positive, integers)
    sources, parity, _ = pair_patches(own, partner)
    group = lax.axis_index("pages")
    count = integers[pl.ds(parity, 1), :block_rows][:, :lanes]
    blocks = [mine[0]] + [ref[0] for ref in fetched]
    queries = [group] + [
        group ^ jnp.where(parity == 0, first, second)
        for first, second in zip(*[side[: len(fetched)] for side in fetches])
    ]
    mean, highest, total = page_softmax(
        jnp.concatenate(blocks, axis=0), sources, parity, count, scores
    )
    means[...] = mean.reshape(means.shape)
    for i, rows in enumerate(query_rows((highest, total), queries)):
        lines[i] = rows


def late_kernel(
    share, integers, own, partner, early_means, early_lines, mine, *refs
):
    fetched, others, (out, tokens, scores) = refs[:-4], refs[-4], refs[-3:]
    sources, parity, first_slot = pair_patches(own, partner)
    group = lax.axis_index("pages")
    count = integers[pl.ds(parity, 1), :block_rows][:, :lanes]
    near = len(fetched) - 1
    blocks = [jnp.where(parity == 1, fetched[near][0], others[near])]
    blocks = blocks + [others[i] for i in range(near)]
    early_blocks = [mine[0]] + [ref[0] for ref in fetched[:near]]
    early_queries, queries = [group], [group ^ fetches[1][near]]
    for first, second in zip(*[side[:near] for side in fetches]):
        early_queries.append(group ^ jnp.where(parity == 0, first, second))
        queries.append(group ^ jnp.where(parity == 0, second, first))
    mean, highest, total = page_softmax(
        jnp.concatenate(blocks, axis=0), sources, parity, count, scores
    )
    query_len = blocks[0].shape[0]
    lines = out.shape[1] * share // query_len
    for i, query in enumerate(queries):
        tokens[pl.ds(query, 1)] = blocks[i][None]
        tokens[pl.ds(early_queries[i], 1)] = early_blocks[i][None]
        for k in range(query_len // share):
            part = mean[i * query_len + k * share : i * query_len + (k + 1) * share]
            place = (slice(k * lines, k * lines + share), slice(None))
            out[(pl.ds(query, 1), *place)] = part[None]
            part = early_means[i, k * share : (k + 1) * share]
            out[(pl.ds(early_queries[i], 1), *place)] = part[None]
    highest, total = query_rows((highest, total), queries)
    highest, total = highest + early_lines[0], total + early_lines[1]
    smooth = highest + smooth_tau * (jnp.log(total) - jnp.log(count.astype(jnp.float32)))
    smooth = jnp.where(count > first_slot, smooth, neg_large)
    for half in range(smooth.shape[0]):
        row = jnp.broadcast_to(smooth[half : half + 1][None], (out.shape[0], 1, lanes))
        for k in range(query_len // share):
            line = k * lines + share + half
            out[:, line : line + 1] = row


def forward_kernel(share, lines, integers, tokens, own, partner, out, scores):
    block_peers = block_rows // share
    peers = out.shape[0] // lines
    pair_pages = own.shape[0] // 2
    sources, parity, first_slot = pair_patches(own, partner)
    diagonal = lax.broadcasted_iota(jnp.int32, (lanes, lanes), 0) == lax.broadcasted_iota(
        jnp.int32, (lanes, lanes), 1
    )

    def as_row(column):
        return jnp.sum(jnp.where(diagonal, column, 0.0), axis=0, keepdims=True)

    def block(b):
        token_rows = block_of_tokens(tokens, b)
        for index in range(pair_pages):
            page = parity * pair_pages + index
            count = integers[pl.ds(page, 1), :block_rows][:, :lanes]
            mean, highest, total = page_softmax(token_rows, sources, page, count, scores)
            for i in range(block_peers):
                line = (b * block_peers + i) * lines + index * share
                out[pl.ds(line, share)] = mean[i * share : (i + 1) * share]
            log_count = jnp.log(count.astype(jnp.float32))
            for half in range(block_rows // lanes):
                rows = slice(half * lanes, (half + 1) * lanes)
                log_mean = jnp.log(as_row(total[rows])) - log_count
                smooth = as_row(highest[rows]) + smooth_tau * log_mean
                smooth = jnp.where(count > first_slot, smooth, neg_large)
                line = pair_pages * share + (b * pair_pages + index) * (block_rows // lanes) + half
                out[pl.ds(line, peers, stride=lines)] = jnp.broadcast_to(smooth, (peers, lanes))

    over_blocks(tokens.shape[0] * tokens.shape[1] // block_rows, block)


def backward_kernel(
    slots, share, lines, integers, heard, tokens, own, loss, query_grad, page_grad
):
    page_local, patch_local, width = own.shape
    query_len = tokens.shape[1]
    block_queries = block_rows // query_len
    halves = block_rows // lanes
    half_queries = lanes // query_len
    pair_pages = page_local // 2
    groups = heard.shape[0] // (lines * slots)
    sides = slots // 2
    slot = lax.axis_index("queries")
    group = lax.axis_index("pages")
    same_query = (
        lax.broadcasted_iota(jnp.int32, (lanes, lanes), 0) // query_len
        == lax.broadcasted_iota(jnp.int32, (lanes, lanes), 1) // query_len
    ).astype(jnp.bfloat16)
    group_ids = lax.broadcasted_iota(jnp.int32, (groups, lanes), 0)
    position = lax.broadcasted_iota(jnp.int32, (patch_local, block_rows), 0)
    pages = range(page_local)

    def sender(page, side):
        return 2 * side + page // pair_pages

    def token_sums(x):
        coarse = x.astype(jnp.bfloat16)
        rest = x - coarse.astype(jnp.float32)
        middle = rest.astype(jnp.bfloat16)
        fine = (rest - middle.astype(jnp.float32)).astype(jnp.bfloat16)
        sums = contract(jnp.concatenate([coarse, middle, fine], axis=0), same_query, 1, 0)
        size = x.shape[0]
        return sums[:size] + sums[size : 2 * size] + sums[2 * size :]

    def mine(x):
        return jnp.sum(jnp.where(group_ids == group, x, 0.0), axis=0, keepdims=True)

    def block(b):
        row_weights = [[] for _ in pages]
        row_lse = [[] for _ in pages]
        shares = []
        smooths, all_parts = [], []
        for half in range(halves):
            smooth = []
            parts = []
            for page in pages:
                line = pair_pages * share + (b * pair_pages + page % pair_pages) * halves + half
                heights = [
                    heard[pl.ds(sender(page, side) * lines + line, groups, stride=slots * lines)]
                    for side in range(sides)
                ]
                highest = functools.reduce(jnp.maximum, heights)
                terms = [jnp.exp2((x - highest) * inv_tau_log2) for x in heights]
                total = functools.reduce(jnp.add, terms)
                smooth.append(highest + smooth_tau * jnp.log(total))
                inverse = 1.0 / total
                parts.append([x * inverse for x in terms])
            smooths.append(smooth)
            all_parts.append(parts)
        every = token_sums(jnp.concatenate([x for smooth in smooths for x in smooth], axis=0))
        for half, (smooth, parts) in enumerate(zip(smooths, all_parts)):
            first = half * page_local * groups
            sums = every[first : first + page_local * groups] * inv_temp
            logits = [sums[page * groups : (page + 1) * groups] for page in pages]
            top = functools.reduce(jnp.maximum, logits)
            top = jnp.max(top, axis=0, keepdims=True)
            grown = [jnp.exp(x - top) for x in logits]
            total = jnp.sum(functools.reduce(jnp.add, grown), axis=0, keepdims=True)
            first_query = b * block_queries + half * half_queries
            line = pl.multiple_of(first_query * query_len, lanes)
            target = integers[page_local : page_local + 1, pl.ds(line, lanes)]
            hits = [group_ids * page_local + page == target for page in pages]
            found = functools.reduce(
                jnp.add, [jnp.where(hit, x, 0.0) for hit, x in zip(hits, logits)]
            )
            losses = top + jnp.log(total) - jnp.sum(found, axis=0, keepdims=True)
            for i in range(half_queries):
                loss[first_query + i] = jnp.max(losses[:, i * query_len : (i + 1) * query_len])
            inverse = 1.0 / total
            weights = [
                (x * inverse - jnp.where(hit, 1.0, 0.0)) * inv_temp for hit, x in zip(hits, grown)
            ]
            for page in pages:
                row_weights[page].append(mine(weights[page]))
                row_lse[page].append(mine(smooth[page]))
            shares.append([[weights[page] * part for part in parts[page]] for page in pages])

        token_rows = block_of_tokens(tokens, b)
        for page in pages:
            count = integers[page : page + 1, :block_rows]
            live_count = count - slot * patch_local
            page_weight = jnp.concatenate(row_weights[page], axis=1)
            page_lse = jnp.concatenate(row_lse[page], axis=1) + smooth_tau * log_row(count)
            similar = contract(own[page], token_rows, 1, 1)
            coef = page_weight * jnp.exp2((similar - page_lse) * inv_tau_log2)
            coef = jnp.where(position < live_count, coef, 0.0).astype(jnp.bfloat16)
            grad = contract(coef, token_rows, 1, 0)
            if tokens.shape[0] > block_queries:
                grad = grad + jnp.where(b == 0, 0.0, page_grad[page])
            page_grad[page] = grad

        def own_rows():
            row = lax.rem(group, block_queries) * query_len + slot * share
            picked = []
            for page in pages:
                for side in range(sides):
                    x = shares[0][page][side]
                    for other in range(1, halves):
                        x = jnp.where(row // lanes == other, shares[other][page][side], x)
                    picked.append(x)
            picked = jnp.concatenate(picked, axis=0)
            picked = pltpu.roll(picked, lax.rem(lanes - lax.rem(row, lanes), lanes), 1)
            columns = jnp.transpose(picked)[:share]
            grads = []
            for page in pages:
                for side in range(sides):
                    place = len(grads) * groups
                    first = sender(page, side) * lines + page % pair_pages * share
                    terms = [
                        columns[:, place + g : place + g + 1]
                        * heard[first + g * slots * lines : first + g * slots * lines + share]
                        for g in range(groups)
                    ]
                    grads.append(functools.reduce(jnp.add, terms))
            query_grad[0] = functools.reduce(jnp.add, grads)

        if tokens.shape[0] == block_queries:
            own_rows()
        else:
            pl.when(group // block_queries == b)(own_rows)

    over_blocks(tokens.shape[0] // block_queries, block)


def fetch_pairs(page_groups, slots, index):
    return [
        (group * slots + slot, (group ^ shift) * slots + slot)
        for slot in range(slots)
        for shift in fetches[slot % 2][index : index + 1]
        for group in range(page_groups)
    ]


def shards(page_groups, slots, query_tokens, page_patches, patch_counts, positive_page):
    query_local, query_len, width = query_tokens.shape
    page_local, patch_local, _ = page_patches.shape
    query_count = query_local * page_groups
    share = query_len // slots
    peers = page_groups * slots
    lines = page_local // 2 * (share + query_count * query_len // lanes)
    tile = math.gcd(lines, 8)
    smem = pl.BlockSpec(memory_space=pltpu.SMEM)
    vmem = pl.BlockSpec(memory_space=pltpu.VMEM)
    limit = (16 << 20) + 2 * peers * lines * lanes * 4
    params = pltpu.CompilerParams(vmem_limit_bytes=limit)

    partner = lax.ppermute(page_patches, "queries", [(i, i ^ 1) for i in range(slots)])
    token_shape = jax.ShapeDtypeStruct((page_groups, query_len, width), query_tokens.dtype)
    told_shape = jax.ShapeDtypeStruct((peers * lines, lanes), jnp.float32)
    scores = pltpu.VMEM((2, block_rows, patch_local), jnp.float32)
    small = pltpu.CompilerParams(vmem_limit_bytes=4 << 20)
    integer_shape = jax.ShapeDtypeStruct((page_local + 1, query_count * query_len), jnp.int32)
    if page_local == 2 and page_groups == 1 + sum(len(side) for side in fetches):
        fetched = [
            lax.ppermute(query_tokens, both, fetch_pairs(page_groups, slots, i))
            for i in range(len(fetches[1]))
        ]
        held = pl.pallas_call(
            hold_kernel,
            out_shape=jax.ShapeDtypeStruct(page_patches.shape, page_patches.dtype),
            in_specs=[vmem],
            out_specs=vmem,
            compiler_params=small,
            name="hold",
        )(page_patches)
        gathered = pl.pallas_call(
            gather_kernel,
            out_shape=jax.ShapeDtypeStruct((len(fetched), query_len, width), query_tokens.dtype),
            in_specs=[vmem] * (len(fetched) + 1),
            out_specs=vmem,
            compiler_params=small,
            name="gather",
        )(held, *fetched)
        others = lax.ppermute(gathered, "queries", [(i, i ^ 1) for i in range(slots)])
        near = len(fetched) - 1
        half_scores = pltpu.VMEM((2, block_rows // 2, patch_local), jnp.float32)
        means, rows, integers = pl.pallas_call(
            early_kernel,
            out_shape=(
                jax.ShapeDtypeStruct((near + 1, query_len, width), jnp.float32),
                jax.ShapeDtypeStruct((2, block_rows // lanes, lanes), jnp.float32),
                integer_shape,
            ),
            in_specs=[vmem] * (5 + near),
            out_specs=(vmem, vmem, vmem),
            scratch_shapes=[half_scores],
            compiler_params=params,
            name="early",
        )(patch_counts, positive_page, held, partner, query_tokens, *fetched[:near])
        told, tokens = pl.pallas_call(
            functools.partial(late_kernel, share),
            out_shape=(
                jax.ShapeDtypeStruct((page_groups, slots * lines, lanes), jnp.float32),
                token_shape,
            ),
            in_specs=[vmem] * (7 + len(fetched)),
            out_specs=(vmem, vmem),
            scratch_shapes=[half_scores],
            compiler_params=params,
            name="late",
        )(integers, held, partner, means, rows, query_tokens, *fetched, others)
    else:
        tokens = lax.all_to_all(
            jnp.broadcast_to(query_tokens, token_shape.shape), "pages", 0, 0, tiled=True
        )
        held = page_patches
        integers = pl.pallas_call(
            integer_rows,
            out_shape=integer_shape,
            in_specs=[vmem] * 2,
            out_specs=vmem,
            compiler_params=small,
            name="integers",
        )(patch_counts, positive_page)
        told = pl.pallas_call(
            functools.partial(forward_kernel, share, lines),
            out_shape=told_shape,
            in_specs=[vmem] * 4,
            out_specs=vmem,
            scratch_shapes=[scores],
            compiler_params=params,
            name="forward",
        )(integers, tokens, held, partner)
    told = told.reshape(peers, lines // tile, tile, lanes)
    heard = lax.all_to_all(told, both, 0, 0, tiled=True).reshape(peers * lines, lanes)
    return pl.pallas_call(
        functools.partial(backward_kernel, slots, share, lines),
        out_shape=(
            jax.ShapeDtypeStruct((query_count,), jnp.float32),
            jax.ShapeDtypeStruct((query_local, share, width), jnp.float32),
            jax.ShapeDtypeStruct((page_local, patch_local, width), jnp.float32),
        ),
        in_specs=[vmem] * 4,
        out_specs=(smem, vmem, vmem),
        compiler_params=params,
        name="backward",
    )(integers, heard, tokens, held)


def solution(mesh):
    in_specs = (P("pages", None, None), P("pages", "queries", None), P("pages"), P())
    out_specs = (P(), P("pages", "queries", None), P("pages", "queries", None))
    body = functools.partial(shards, mesh.shape["pages"], mesh.shape["queries"])
    return jax.shard_map(body, mesh=mesh, in_specs=in_specs, out_specs=out_specs, check_vma=False)
```
